32 devices in a mesh: gx: 4 (over z), gz: 8 (over y, x, core).
Axes of the slice: x: 2, y: 2, z: 4, core: 2. Of those that a mesh axis runs over, the one named last changes fastest.
Arguments:
- velocity: float32 [3, 4096, 1, 4096], P(None, 'gx', None, 'gz'), may hold values from -6 to 6
Outputs:
- advection: float32 [3, 4096, 1, 4096], P(None, 'gx', None, 'gz')
The draws below stay inside these ranges and needn't reach their ends.
All inputs are finite; a program needn't handle non-finite values.
Results may differ from the reference program's by a relative error of at most 0.00013.
Values sent between devices are 32-bit elements; how exact they have to be, the bound alone decides.
No kernel may reach another device: no remote copies, remote signals or barrier semaphores. Data moves between devices by JAX's collectives and lax.ppermute only.
A program may use at most 128 MiB of HBM per device.

```python
import jax
import jax.numpy as jnp
from jax import lax

NX = 4096
NZ = 4096
YP = 1


def steps_of(key, shape, shards, least, top_value):
    def one(position, parts):
        draws = jax.random.uniform(jax.random.fold_in(jax.random.fold_in(key, 6), position), (parts,), jnp.float32, least / len(shards), top_value / len(shards))
        return jnp.repeat(jnp.exp(draws), shape[position] // parts).reshape((-1,) + (1,) * (len(shape) - position - 1))

    loudness = one(*shards[0])
    for cut in shards[1:]:
        loudness = loudness * one(*cut)
    return loudness


def scatter_about(own_key, shape, deviation, bound, split=(), kind=jnp.bfloat16):
    entries = deviation * jax.random.normal(own_key, shape, jnp.float32)
    if split:
        entries = entries * steps_of(own_key, shape, split, -0.22, 0.18)
    return jnp.clip(entries, -bound, bound).astype(kind)


def setup_inputs(seed: int = 0) -> dict:
    key_list = jax.random.split(jax.random.key(seed), 2)
    return {
        "velocity": scatter_about(key_list[0], (3, NX, YP, NZ), 1.0, 6.0, ((1, 4), (3, 8)), jnp.float32),
    }


ALPHA_D = 1.0 / 3.0
COEF_A = 14.0 / 9.0
COEF_B = 1.0 / 9.0
ALPHA_F = 0.49


def filter_coefficients():
    return ((11.0 + 10.0 * ALPHA_F) / 16.0, (15.0 + 34.0 * ALPHA_F) / 32.0,
            (-3.0 + 6.0 * ALPHA_F) / 16.0, (1.0 - 2.0 * ALPHA_F) / 32.0)


def shifted(values, offset, direction):
    return jnp.roll(values, -offset, axis=direction)


def circulant_solve(rhs, alpha, direction):
    length = rhs.shape[direction]
    spectrum = jnp.fft.rfft(rhs, axis=direction)
    wavenums = jnp.arange(length // 2 + 1, dtype=jnp.float32)
    symbol = 1.0 + 2.0 * alpha * jnp.cos(2.0 * jnp.pi * wavenums / length)
    dims_list = [1] * rhs.ndim
    dims_list[direction] = length // 2 + 1
    return jnp.fft.irfft(spectrum / symbol.reshape(dims_list), n=length, axis=direction).astype(rhs.dtype)


def slope(values, direction):
    rhs = COEF_A * 0.5 * (shifted(values, 1, direction) - shifted(values, -1, direction))
    rhs = rhs + COEF_B * 0.25 * (shifted(values, 2, direction) - shifted(values, -2, direction))
    return circulant_solve(rhs, ALPHA_D, direction)


def smooth(values, direction):
    coefficients = filter_coefficients()
    rhs = coefficients[0] * values
    for offset in range(1, 4):
        rhs = rhs + 0.5 * coefficients[offset] * (shifted(values, offset, direction) + shifted(values, -offset, direction))
    return circulant_solve(rhs, ALPHA_F, direction)


def one_plane(velocity_plane):
    along_x = velocity_plane[0:1]
    along_z = velocity_plane[2:3]
    x_terms = slope(along_x * velocity_plane, 1) + along_x * slope(velocity_plane, 1)
    z_terms = slope(along_z * velocity_plane, 2) + along_z * slope(velocity_plane, 2)
    return -smooth(0.5 * (x_terms + z_terms), 1)


def reference(velocity):
    planes = lax.map(one_plane, jnp.moveaxis(velocity, 2, 0))
    return jnp.moveaxis(planes, 0, 2)
```

```python
import functools

import numpy as np
import ml_dtypes
import jax
import jax.numpy as jnp
from jax import lax
from jax.experimental import pallas as pl
from jax.experimental.pallas import tpu as pltpu
from jax.sharding import PartitionSpec as P

ALPHA_D = 1.0 / 3.0
COEF_A = 14.0 / 9.0
COEF_B = 1.0 / 9.0
ALPHA_F = 0.49
block_len = 128

LANES = 128
SUBLANES = 8
REACH_D = 24
REACH_F = 96

ROOT_D = (-1.0 + np.sqrt(1.0 - 4.0 * ALPHA_D**2)) / (2.0 * ALPHA_D)
NEAR_D = COEF_B / (4.0 * ALPHA_D)
GAIN_D = (COEF_A / 2.0 - NEAR_D) * (1.0 - ROOT_D**2) / np.sqrt(1.0 - 4.0 * ALPHA_D**2)
BETA = NEAR_D / GAIN_D


def filter_coefficients():
    return (
        (11.0 + 10.0 * ALPHA_F) / 16.0,
        (15.0 + 34.0 * ALPHA_F) / 32.0,
        (-3.0 + 6.0 * ALPHA_F) / 16.0,
        (1.0 - 2.0 * ALPHA_F) / 32.0,
    )


def split_filter():
    a0, a1, a2, a3 = filter_coefficients()
    poly = [a0 - a2, 0.5 * a1 - 1.5 * a3, 0.5 * a2, 0.5 * a3]
    tap2 = poly[3] / ALPHA_F
    tap1 = (poly[2] - tap2) / ALPHA_F
    tap0 = (poly[1] - tap1) / ALPHA_F
    rest = poly[0] - tap0
    root = (-1.0 + np.sqrt(1.0 - 4.0 * ALPHA_F**2)) / (2.0 * ALPHA_F)
    gain = rest / np.sqrt(1.0 - 4.0 * ALPHA_F**2)
    return root, gain, (tap0 + 2.0 * tap2) / gain, tap1 / gain, tap2 / gain


ROOT_F, GAIN_F, TAP0, TAP1, TAP2 = (float(v) for v in split_filter())
ROOT_D, GAIN_D, BETA = float(ROOT_D), float(GAIN_D), float(BETA)
SCALE = -0.5 * GAIN_D * GAIN_F


def two_halves(table):
    high = table.astype(ml_dtypes.bfloat16)
    low = (table - high.astype(np.float64)).astype(ml_dtypes.bfloat16)
    return high, low


def line_weights():
    lane = np.arange(LANES)

    def kernel(offset):
        size = np.abs(offset)
        value = np.sign(offset) * (ROOT_D ** (np.maximum(size, 1) - 1.0) + BETA * (size == 1))
        return value

    inside = kernel(lane[:, None] - lane[None, :])
    source = np.where(lane < LANES // 2, lane + LANES, lane - LANES)
    beside = kernel(source[:, None] - lane[None, :])
    rows = []
    for part in (inside, beside):
        high, low = two_halves(part)
        rows += [np.concatenate([high, low], axis=1)] * 2
    return np.concatenate(rows, axis=0)


def end_weights():
    lane = np.arange(LANES)
    rows = []
    for side in range(2):
        for field in range(6):
            table = np.zeros((LANES, LANES))
            if side == 0:
                inner = np.where(lane < LANES - 1, ROOT_D ** (1.0 * np.maximum(LANES - 2 - lane, 0)), 0.0)
                table[:, 2 * field] = inner
                table[LANES - 1, 2 * field + 1] = 1.0
            else:
                inner = np.where(lane > 0, ROOT_D ** (1.0 * np.maximum(lane - 1, 0)), 0.0)
                table[:, 16 + 2 * field + 1] = inner
                table[0, 16 + 2 * field] = 1.0
            high, low = two_halves(table)
            rows += [np.concatenate([high, low], axis=1)] * 2
    return np.concatenate(rows, axis=0)


def split_value(value):
    high = value.astype(jnp.bfloat16)
    low = (value - high.astype(jnp.float32)).astype(jnp.bfloat16)
    return high, low


def low_rows():
    return lax.broadcasted_iota(jnp.int32, (SUBLANES, LANES), 0) < SUBLANES // 2


def six_fields(factor, parts):
    return list(parts) + [factor * part for part in parts]


def ends_kernel(seg, v_ref, w_ref, right_x, left_x, right_z, left_z, xbuf, zbuf, wbuf, xout, zout, sems):
    reach = REACH_D
    copies = []
    for c in range(3):
        copies.append(pltpu.make_async_copy(v_ref.at[c, 0, pl.ds(0, reach)], xbuf.at[c, :, pl.ds(0, 4)], sems.at[4 * c]))
        copies.append(pltpu.make_async_copy(v_ref.at[c, 1, pl.ds(seg - reach, reach)], xbuf.at[c, :, pl.ds(4, 4)], sems.at[4 * c + 1]))
    zcopies = []
    for c in range(3):
        for side in range(2):
            zcopies.append(
                pltpu.make_async_copy(v_ref.at[c, :, :, 3 - 3 * side], zbuf.at[side, c], sems.at[4 * c + 2 + side])
            )
    wcopy = pltpu.make_async_copy(w_ref, wbuf, sems.at[12])
    for copy in copies + zcopies + [wcopy]:
        copy.start()
    for copy in copies:
        copy.wait()
    first = low_rows()
    sums = [jnp.zeros((SUBLANES, LANES), jnp.float32)] * 6
    for k in range(reach):
        weight = jnp.where(first, ROOT_D**k, ROOT_D ** (reach - 1 - k)).astype(jnp.float32)
        parts = [xbuf[c, k] for c in range(3)]
        sums = [total + weight * field for total, field in zip(sums, six_fields(parts[0], parts))]
    for field in range(6):
        xout[field] = sums[field]
    for c in range(3):
        xout[6 + c] = jnp.where(first, xbuf[c, 0], xbuf[c, reach - 1])
    left_x[...] = xout[:, 0:4, :]
    right_x[...] = xout[:, 4:8, :]
    for copy in zcopies + [wcopy]:
        copy.wait()
    rows = 256
    half = seg // rows

    def block(step, _):
        h = step // half
        base = pl.multiple_of((step % half) * rows, rows)
        pieces = []
        for side in range(2):
            parts = [zbuf[side, c, h, pl.ds(base, rows), :] for c in range(3)]
            for field in six_fields(parts[2], parts):
                pieces += list(split_value(field))
        lhs = jnp.concatenate(pieces, axis=1)
        both = jnp.dot(lhs, wbuf[...], preferred_element_type=jnp.float32)
        numbers = both[:, :LANES] + both[:, LANES:]
        for part in range(rows // LANES):
            turned = numbers[part * LANES : (part + 1) * LANES].T
            at = pl.ds(pl.multiple_of(h * seg + base + part * LANES, LANES), LANES)
            right_z[:, at] = turned[0:16]
            left_z[:, at] = turned[16:32]
        return 0

    lax.fori_loop(0, 2 * half, block, 0)


def ends(view, seg):
    weights = jnp.asarray(end_weights())
    xs = jax.ShapeDtypeStruct((9, 4, LANES), jnp.float32)
    zs = jax.ShapeDtypeStruct((16, 2 * seg), jnp.float32)
    hbm = pl.BlockSpec(memory_space=pl.ANY)
    vmem = pl.BlockSpec(memory_space=pltpu.VMEM)
    return pl.pallas_call(
        functools.partial(ends_kernel, seg),
        out_shape=(xs, xs, zs, zs),
        in_specs=[hbm, hbm],
        out_specs=(vmem,) * 4,
        scratch_shapes=[
            pltpu.VMEM((3, REACH_D, SUBLANES, LANES), jnp.float32),
            pltpu.VMEM((2, 3, 2, seg, LANES), jnp.float32),
            pltpu.VMEM(weights.shape, jnp.bfloat16),
            pltpu.VMEM((9, SUBLANES, LANES), jnp.float32),
            pltpu.VMEM((9, SUBLANES, LANES), jnp.float32),
            pltpu.SemaphoreType.DMA((13,)),
        ],
        compiler_params=pltpu.CompilerParams(vmem_limit_bytes=32 * 2**20),
        name="line_ends",
    )(view, weights)


def x_kernel(seg, parts_n, v_ref, s_ref, vbuf, fwd, sems_in, sems_halo, sems_out):
    reach = REACH_D
    size = seg // parts_n

    def load(b):
        out = []
        for c in range(3):
            for h in range(2):
                out.append(
                    pltpu.make_async_copy(
                        v_ref.at[c, h, pl.ds(b * size, size)],
                        vbuf.at[c, pl.ds(reach + b * size, size), pl.ds(4 * h, 4)],
                        sems_in.at[b, 2 * c + h],
                    )
                )
        return out

    def halo(h):
        out = []
        for c in range(3):
            rows = pl.ds(seg - reach, reach) if h == 0 else pl.ds(0, reach)
            at = pl.ds(0, reach) if h == 0 else pl.ds(reach + seg, reach)
            out.append(
                pltpu.make_async_copy(
                    v_ref.at[c, h, rows], vbuf.at[c, at, pl.ds(4 - 4 * h, 4)], sems_halo.at[h, c]
                )
            )
        return out

    def store(b):
        return [
            pltpu.make_async_copy(
                fwd.at[c, pl.ds(b * size, size)], s_ref.at[c, pl.ds(b * size, size)], sems_out.at[b, c]
            )
            for c in range(3)
        ]

    for copy in halo(0):
        copy.start()
    for b in range(parts_n):
        for copy in load(b):
            copy.start()
    for copy in halo(1):
        copy.start()
    vbuf[:, 0:reach, 0:4, :] = jnp.zeros((3, reach, 4, LANES), jnp.float32)
    vbuf[:, reach + seg :, 4:8, :] = jnp.zeros((3, reach, 4, LANES), jnp.float32)
    zero = jnp.zeros((SUBLANES, LANES), jnp.float32)

    def advance(row, carry):
        sums, near = carry
        values = [vbuf[c, row] for c in range(3)]
        terms = six_fields(values[0], values)
        bend = BETA * (near[0] + values[0])
        found = [(sums[3 + c] + values[0] * sums[c]) + near[c] * bend for c in range(3)]
        sums = tuple(term + ROOT_D * total for term, total in zip(terms, sums))
        return found, (sums, tuple(values))

    carry = ((zero,) * 6, (zero,) * 3)
    for copy in halo(0):
        copy.wait()
    carry = lax.fori_loop(0, reach, lambda i, k: advance(i, k)[1], carry, unroll=8)

    def forward(b):
        def body(i, k):
            found, k = advance(reach + b * size + i, k)
            for c in range(3):
                fwd[c, b * size + i] = found[c]
            return k

        return body

    for b in range(parts_n):
        for copy in load(b):
            copy.wait()
        carry = lax.fori_loop(0, size, forward(b), carry, unroll=8)
    for copy in halo(1):
        copy.wait()
    carry = ((zero,) * 6, (zero,) * 3)
    last = reach + seg + reach - 1
    carry = lax.fori_loop(0, reach, lambda i, k: advance(last - i, k)[1], carry, unroll=8)

    def backward(b):
        def body(i, k):
            row = b * size + size - 1 - i
            found, k = advance(reach + row, k)
            for c in range(3):
                fwd[c, row] = found[c] - fwd[c, row]
            return k

        return body

    for b in reversed(range(parts_n)):
        carry = lax.fori_loop(0, size, backward(b), carry, unroll=8)
        for copy in store(b):
            copy.start()
    for b in reversed(range(parts_n)):
        for copy in store(b):
            copy.wait()


def x_part(view, seg):
    parts_n = 8
    hbm = pl.BlockSpec(memory_space=pl.ANY)
    points = 3 * 2 * seg * 4 * LANES
    return pl.pallas_call(
        functools.partial(x_kernel, seg, parts_n),
        out_shape=jax.ShapeDtypeStruct((3, seg, SUBLANES, LANES), jnp.float32),
        in_specs=[hbm],
        out_specs=hbm,
        scratch_shapes=[
            pltpu.VMEM((3, seg + 2 * REACH_D, SUBLANES, LANES), jnp.float32),
            pltpu.VMEM((3, seg, SUBLANES, LANES), jnp.float32),
            pltpu.SemaphoreType.DMA((parts_n, 6)),
            pltpu.SemaphoreType.DMA((2, 3)),
            pltpu.SemaphoreType.DMA((parts_n, 3)),
        ],
        compiler_params=pltpu.CompilerParams(vmem_limit_bytes=32 * 2**20),
        cost_estimate=pl.CostEstimate(flops=60 * points, bytes_accessed=8 * points, transcendentals=0),
        name="x_slopes",
    )(view)


def z_kernel(
    seg, parts_n, v_ref, sx_ref, w_ref, zl_ref, zr_ref, xl_ref, xr_ref,
    o_ref, fl_ref, fr_ref,
    vbuf, sxbuf, sbuf, lhs, turn, halo_hi, halo_lo, edge, sems_v, sems_s, sems_o, sems_m,
):
    reach, far = REACH_D, REACH_F
    size = seg // parts_n
    total = seg + 2 * far
    step_rows = 16
    rows = 2 * step_rows

    def load(b):
        out = [
            pltpu.make_async_copy(
                v_ref.at[c, h, pl.ds(b * size * 4, size * 4)],
                vbuf.at[c, h, pl.ds(b * size * 4, size * 4)],
                sems_v.at[b, 2 * c + h],
            )
            for c in range(3)
            for h in range(2)
        ]
        out += [
            pltpu.make_async_copy(
                sx_ref.at[c, pl.ds(b * size, size)], sxbuf.at[c, pl.ds(b * size, size)], sems_s.at[b, c]
            )
            for c in range(3)
        ]
        return out

    def store(b):
        return [
            pltpu.make_async_copy(
                sxbuf.at[c, pl.ds(b * size, size), pl.ds(4 * h, 4)],
                o_ref.at[c, h, pl.ds(b * size, size)],
                sems_o.at[b, 2 * c + h],
            )
            for c in range(3)
            for h in range(2)
        ]

    for b in range(parts_n):
        for copy in load(b):
            copy.start()
    edge[...] = jnp.zeros_like(edge)
    edges = [
        pltpu.make_async_copy(xl_ref, edge.at[0, :, pl.ds(0, 4)], sems_m.at[0]),
        pltpu.make_async_copy(xr_ref, edge.at[1, :, pl.ds(4, 4)], sems_m.at[1]),
    ]
    for copy in edges:
        copy.start()

    lane = lax.broadcasted_iota(jnp.int32, (LANES, LANES), 1)
    turn[...] = jnp.zeros_like(turn)
    for part in range(2 * seg // LANES):
        at = pl.ds(part * LANES, LANES)
        turn[0:16, :] = zl_ref[:, at]
        turn[16:32, :] = zr_ref[:, at]
        numbers = turn[...].T
        for field in range(6):
            before = pltpu.roll(numbers, LANES - 2 - 2 * field, axis=1)
            after = pltpu.roll(numbers, LANES - 16 - 2 * field, axis=1)
            tile = jnp.where(lane >= LANES - 2, before, jnp.where(lane < 2, after, 0.0))
            high, low = split_value(tile)
            halo_hi[field, at, :] = high
            halo_lo[field, at, :] = low

    low_lane = lax.broadcasted_iota(jnp.int32, (rows, LANES), 1) < LANES // 2

    def s_row(c, row):
        return pl.multiple_of((c * total + row) * SUBLANES, SUBLANES)

    def block(step, _):
        xi = pl.multiple_of(step * step_rows, step_rows)
        along = []
        for n in range(4):
            values = []
            for c in range(3):
                pieces = [
                    vbuf[c, h, pl.ds((xi + 8 * k) * 4 + n, 8, stride=4), :]
                    for h in range(2)
                    for k in range(step_rows // 8)
                ]
                values.append(jnp.concatenate(pieces, axis=0))
            along.append(values)
        for field in range(6):
            halves = []
            for n in range(4):
                value = along[n][field % 3]
                if field >= 3:
                    value = along[n][2] * value
                halves.append(split_value(value))
            for which, halo in ((0, halo_hi), (1, halo_lo)):
                outer = jnp.concatenate(
                    [halo[field, pl.ds(pl.multiple_of(h * seg + xi, 16), step_rows), :] for h in range(2)], axis=0
                )
                line = [outer] + [pair[which] for pair in halves] + [outer]
                for n in range(4):
                    at = pl.ds((field * 4 + n) * rows, rows)
                    lhs[at, which * LANES : (which + 1) * LANES] = line[n + 1]
                    lhs[at, (2 + which) * LANES : (3 + which) * LANES] = jnp.where(
                        low_lane, line[n + 2], line[n]
                    )
        both = jnp.dot(lhs[...], w_ref[...], preferred_element_type=jnp.float32)
        slopes = both[:, :LANES] + both[:, LANES:]
        for c in range(3):
            for n in range(4):
                plain = slopes[(c * 4 + n) * rows : (c * 4 + n + 1) * rows]
                mixed = slopes[((3 + c) * 4 + n) * rows : ((3 + c) * 4 + n + 1) * rows]
                term = mixed + along[n][2] * plain
                for h in range(2):
                    for k in range(step_rows // 8):
                        at = (c * total + far + xi + 8 * k) * SUBLANES + 4 * h + n
                        piece = h * (step_rows // 8) + k
                        sbuf[pl.ds(at, 8, stride=8), :] = term[piece * 8 : piece * 8 + 8]
        for c in range(3):
            at = pl.ds(s_row(c, far + xi), step_rows * SUBLANES)
            sbuf[at, :] = sbuf[at, :] + sxbuf[c, pl.ds(xi, step_rows)].reshape(step_rows * SUBLANES, LANES)
        return 0

    per = size // step_rows
    for b in range(parts_n):
        for copy in load(b):
            copy.wait()
        lax.fori_loop(b * per, (b + 1) * per, block, 0)
    for copy in edges:
        copy.wait()

    def natural(c, row):
        first = vbuf[c, 0, pl.ds(row * 4, 4), :]
        second = vbuf[c, 1, pl.ds(row * 4, 4), :]
        return jnp.concatenate([first, second], axis=0)

    for side in range(2):
        for k in range(reach):
            row = k if side == 0 else seg - 1 - k
            sign = -1.0 if side == 0 else 1.0
            u = natural(0, row)
            for c in range(3):
                add = ROOT_D**k * (edge[side, 3 + c] + u * edge[side, c])
                if k == 0:
                    add = add + BETA * edge[side, 6 + c] * (edge[side, 6] + u)
                at = pl.ds(s_row(c, far + row), SUBLANES)
                sbuf[at, :] = sbuf[at, :] + sign * add

    first = low_rows()

    def wrap(k, _):
        for c in range(3):
            end = sbuf[pl.ds(s_row(c, seg + k), SUBLANES), :]
            sbuf[pl.ds(s_row(c, k), SUBLANES), :] = jnp.where(first, 0.0, pltpu.roll(end, 4, axis=0))
            start = sbuf[pl.ds(s_row(c, far + k), SUBLANES), :]
            sbuf[pl.ds(s_row(c, far + seg + k), SUBLANES), :] = jnp.where(first, pltpu.roll(start, 4, axis=0), 0.0)
        return 0

    lax.fori_loop(0, far, wrap, 0, unroll=4)

    zero = jnp.zeros((SUBLANES, LANES), jnp.float32)

    def row_of(c, row):
        return sbuf[pl.ds(s_row(c, row), SUBLANES), :]

    def sweep(row, sums):
        return tuple(row_of(c, row) + ROOT_F * sums[c] for c in range(3))

    sums = lax.fori_loop(0, far, sweep, (zero,) * 3, unroll=8)

    def forward(i, sums):
        scaled = [ROOT_F * sums[c] for c in range(3)]
        for c in range(3):
            sxbuf[c, i] = scaled[c]
        return tuple(row_of(c, far + i) + scaled[c] for c in range(3))

    sums = lax.fori_loop(0, seg, forward, sums, unroll=8)
    for c in range(3):
        fr_ref[c] = sums[c][4:8]
        fr_ref[3 + c] = row_of(c, far + seg - 1)[4:8]
        fr_ref[6 + c] = row_of(c, far + seg - 2)[4:8]

    sums = lax.fori_loop(0, far, lambda i, k: sweep(total - 1 - i, k), (zero,) * 3, unroll=8)

    def backward(b):
        def body(i, sums):
            row = b * size + size - 1 - i
            out = []
            for c in range(3):
                here = row_of(c, far + row)
                up = here + ROOT_F * sums[c]
                taps = TAP0 * here + TAP1 * (row_of(c, far + row + 1) + row_of(c, far + row - 1))
                taps = taps + TAP2 * (row_of(c, far + row + 2) + row_of(c, far + row - 2))
                sxbuf[c, row] = SCALE * (up + sxbuf[c, row] + taps)
                out.append(up)
            return tuple(out)

        return body

    for b in reversed(range(parts_n)):
        sums = lax.fori_loop(0, size, backward(b), sums, unroll=8)
        for copy in store(b):
            copy.start()
    for c in range(3):
        fl_ref[c] = sums[c][0:4]
        fl_ref[3 + c] = row_of(c, far)[0:4]
        fl_ref[6 + c] = row_of(c, far + 1)[0:4]
    for b in reversed(range(parts_n)):
        for copy in store(b):
            copy.wait()


def z_part(view, local, seg, from_left_z, from_right_z, from_left_x, from_right_x):
    parts_n = 8
    hbm = pl.BlockSpec(memory_space=pl.ANY)
    vmem = pl.BlockSpec(memory_space=pltpu.VMEM)
    weights = jnp.asarray(line_weights())
    ends_shape = jax.ShapeDtypeStruct((9, 4, LANES), jnp.float32)
    total = seg + 2 * REACH_F
    return pl.pallas_call(
        functools.partial(z_kernel, seg, parts_n),
        out_shape=(jax.ShapeDtypeStruct((3, 2, seg, 4, LANES), jnp.float32), ends_shape, ends_shape),
        in_specs=[hbm, hbm, vmem, vmem, vmem, hbm, hbm],
        out_specs=(hbm, vmem, vmem),
        scratch_shapes=[
            pltpu.VMEM((3, 2, seg * 4, LANES), jnp.float32),
            pltpu.VMEM((3, seg, SUBLANES, LANES), jnp.float32),
            pltpu.VMEM((3 * total * SUBLANES, LANES), jnp.float32),
            pltpu.VMEM((24 * 32, 4 * LANES), jnp.bfloat16),
            pltpu.VMEM((LANES, LANES), jnp.float32),
            pltpu.VMEM((6, 2 * seg, LANES), jnp.bfloat16),
            pltpu.VMEM((6, 2 * seg, LANES), jnp.bfloat16),
            pltpu.VMEM((2, 9, SUBLANES, LANES), jnp.float32),
            pltpu.SemaphoreType.DMA((parts_n, 6)),
            pltpu.SemaphoreType.DMA((parts_n, 3)),
            pltpu.SemaphoreType.DMA((parts_n, 6)),
            pltpu.SemaphoreType.DMA((2,)),
        ],
        compiler_params=pltpu.CompilerParams(vmem_limit_bytes=48 * 2**20),
        name="z_slopes_and_filter",
    )(view.reshape(3, 2, seg * 4, LANES), local, weights, from_left_z, from_right_z, from_left_x, from_right_x)


def rim_kernel(seg, o_in, left_ref, right_ref, o_ref, buf, edge, sems, sems_o, sems_m):
    del o_in
    far = REACH_F

    def rows(c, h):
        return o_ref.at[c, h, pl.ds(0, far)] if h == 0 else o_ref.at[c, h, pl.ds(seg - far, far)]

    loads = [
        pltpu.make_async_copy(rows(c, h), buf.at[c, :, pl.ds(4 * h, 4)], sems.at[c, h])
        for c in range(3)
        for h in range(2)
    ]
    loads.append(pltpu.make_async_copy(left_ref, edge.at[:, pl.ds(0, 4)], sems_m.at[0]))
    loads.append(pltpu.make_async_copy(right_ref, edge.at[:, pl.ds(4, 4)], sems_m.at[1]))
    stores = [
        pltpu.make_async_copy(buf.at[c, :, pl.ds(4 * h, 4)], rows(c, h), sems_o.at[c, h])
        for c in range(3)
        for h in range(2)
    ]
    for copy in loads:
        copy.start()
    for copy in loads:
        copy.wait()
    first = low_rows()
    sums = [edge[c] for c in range(3)]
    for k in range(far):
        weight = jnp.where(first, SCALE * ROOT_F ** (k + 1), SCALE * ROOT_F ** (far - k)).astype(jnp.float32)
        for c in range(3):
            buf[c, k] = buf[c, k] + weight * sums[c]
    for c in range(3):
        one, two = edge[3 + c], edge[6 + c]
        outer = SCALE * (TAP1 * one + TAP2 * two)
        inner = (SCALE * TAP2) * one
        buf[c, 0] = buf[c, 0] + jnp.where(first, outer, 0.0)
        buf[c, 1] = buf[c, 1] + jnp.where(first, inner, 0.0)
        buf[c, far - 1] = buf[c, far - 1] + jnp.where(first, 0.0, outer)
        buf[c, far - 2] = buf[c, far - 2] + jnp.where(first, 0.0, inner)
    for copy in stores:
        copy.start()
    for copy in stores:
        copy.wait()


def rim_part(out, left, right, seg):
    hbm = pl.BlockSpec(memory_space=pl.ANY)
    return pl.pallas_call(
        functools.partial(rim_kernel, seg),
        out_shape=jax.ShapeDtypeStruct(out.shape, jnp.float32),
        in_specs=[hbm, hbm, hbm],
        out_specs=hbm,
        input_output_aliases={0: 0},
        scratch_shapes=[
            pltpu.VMEM((3, REACH_F, SUBLANES, LANES), jnp.float32),
            pltpu.VMEM((9, SUBLANES, LANES), jnp.float32),
            pltpu.SemaphoreType.DMA((3, 2)),
            pltpu.SemaphoreType.DMA((3, 2)),
            pltpu.SemaphoreType.DMA((2,)),
        ],
        compiler_params=pltpu.CompilerParams(vmem_limit_bytes=16 * 2**20),
        name="rim",
    )(out, left, right)


def ring(axis):
    count = lax.axis_size(axis)
    forward = [(i, (i + 1) % count) for i in range(count)]
    return forward, [(target, source) for source, target in forward]


def swap_ends(right, left, axis):
    forward, backward = ring(axis)
    return lax.ppermute(right, axis, forward), lax.ppermute(left, axis, backward)


def blocked(velocity):
    seg = velocity.shape[1] // 2
    view = velocity.reshape(3, 2, seg, 4, LANES)
    right_x, left_x, right_z, left_z = ends(view, seg)
    before_x, after_x = swap_ends(right_x, left_x, "gx")
    before_z, after_z = swap_ends(right_z, left_z, "gz")
    local = x_part(view, seg)
    out, left_f, right_f = z_part(view, local, seg, before_z, after_z, before_x, after_x)
    before_f, after_f = swap_ends(right_f, left_f, "gx")
    return rim_part(out, before_f, after_f, seg).reshape(velocity.shape)


def with_halo(block, sides, width):
    for axis, dim in sides:
        count = lax.axis_size(axis)
        forward = [(i, i + 1) for i in range(count - 1)]
        forward.append((count - 1, 0))
        backward = [(target, source) for source, target in forward]
        low = lax.ppermute(
            lax.slice_in_dim(block, block.shape[dim] - width, None, axis=dim), axis, forward
        )
        high = lax.ppermute(lax.slice_in_dim(block, 0, width, axis=dim), axis, backward)
        block = jnp.concatenate([low, block, high], axis=dim)
    return block


def tables(length, alpha):
    lower_diag = jnp.concatenate(
        [jnp.zeros((1,), jnp.float32), jnp.full((length - 1,), alpha, jnp.float32)]
    )
    upper_diag = jnp.concatenate(
        [jnp.full((length - 1,), alpha, jnp.float32), jnp.zeros((1,), jnp.float32)]
    )
    main_diag = jnp.ones((length,), jnp.float32)
    identity = jnp.eye(length, dtype=jnp.float32)
    inverse = lax.linalg.tridiagonal_solve(lower_diag, main_diag, upper_diag, identity)
    left_col = alpha * inverse[:, 0]
    right_col = alpha * inverse[:, length - 1]
    coupling = alpha * inverse[0, 0]
    return (inverse, left_col, right_col, coupling)


def offset_slice(extended, offset, length, direction, base=3):
    return lax.slice_in_dim(extended, base + offset, base + offset + length, axis=direction)


def slope_rhs(extended, length, direction, base=3):
    rhs = (
        COEF_A
        * 0.5
        * (
            offset_slice(extended, 1, length, direction, base)
            - offset_slice(extended, -1, length, direction, base)
        )
    )
    return rhs + COEF_B * 0.25 * (
        offset_slice(extended, 2, length, direction, base)
        - offset_slice(extended, -2, length, direction, base)
    )


def smooth_rhs(extended, length, direction, base=3):
    coefficients = filter_coefficients()
    rhs = coefficients[0] * offset_slice(extended, 0, length, direction, base)
    for offset in range(1, 4):
        rhs = rhs + 0.5 * coefficients[offset] * (
            offset_slice(extended, offset, length, direction, base)
            + offset_slice(extended, -offset, length, direction, base)
        )
    return rhs


def wrap_pad(values, direction):
    length = values.shape[direction]
    return jnp.concatenate(
        [
            lax.slice_in_dim(values, length - 3, length, axis=direction),
            values,
            lax.slice_in_dim(values, 0, 3, axis=direction),
        ],
        axis=direction,
    )


def apply_along(inverse, values, direction):
    rotated = jnp.tensordot(
        inverse, values, axes=([1], [direction]), precision=lax.Precision.HIGHEST
    )
    return jnp.moveaxis(rotated, 0, direction)


def end_values(partial_value, direction):
    length = partial_value.shape[direction]
    first_val = lax.slice_in_dim(partial_value, 0, 1, axis=direction)
    last_val = lax.slice_in_dim(partial_value, length - 1, length, axis=direction)
    return (first_val, last_val)


def corrected(partial_value, prev_last, next_first, table, direction):
    inverse, left_col, right_col, coupling = table
    first_val, last_val = end_values(partial_value, direction)
    factor_inv = 1.0 / (1.0 - coupling * coupling)
    left_value = (prev_last - coupling * first_val) * factor_inv
    right_value = (next_first - coupling * last_val) * factor_inv
    dims_list = [1] * partial_value.ndim
    dims_list[direction] = partial_value.shape[direction]
    return (
        partial_value
        - left_col.reshape(dims_list) * left_value
        - right_col.reshape(dims_list) * right_value
    )


def extend_x(values):
    return with_halo(values, (("gx", 1),), 3)


def solve_x(rhs, table):
    partial_value = apply_along(table[0], rhs, 1)
    first_val, last_val = end_values(partial_value, 1)
    beside = with_halo(jnp.concatenate([first_val, last_val], axis=1), (("gx", 1),), 1)
    return corrected(partial_value, beside[:, 0:1], beside[:, 3:4], table, 1)


def solve_blocks(rhs, table):
    dims_list = rhs.shape
    blocks = rhs.reshape(dims_list[:-1] + (dims_list[-1] // block_len, block_len))
    last_dim = blocks.ndim - 1
    partial_value = apply_along(table[0], blocks, last_dim)
    first_val, last_val = end_values(partial_value, last_dim)
    prev_last = jnp.roll(last_val, 1, axis=last_dim - 1)
    next_first = jnp.roll(first_val, -1, axis=last_dim - 1)
    return corrected(partial_value, prev_last, next_first, table, last_dim).reshape(dims_list)


def whole_z_part(velocity):
    slope_z = tables(block_len, ALPHA_D)
    pencil = lax.all_to_all(velocity, "gz", split_axis=1, concat_axis=3, tiled=True)
    along_z = pencil[2:3]
    fields = jnp.concatenate([pencil, along_z * pencil], axis=0)
    slopes = solve_blocks(slope_rhs(wrap_pad(fields, 3), fields.shape[3], 3), slope_z)
    local_terms = slopes[3:] + along_z * slopes[:3]
    return lax.all_to_all(local_terms, "gz", split_axis=3, concat_axis=1, tiled=True)


def per_device(velocity):
    width_x = velocity.shape[1]
    slope_x = tables(width_x, ALPHA_D)
    smooth_x = tables(width_x, ALPHA_F)
    along_x = velocity[0:1]
    rim_source = jnp.concatenate([velocity, along_x * velocity], axis=0)
    padded = extend_x(rim_source)
    slopes_x = solve_x(slope_rhs(padded, width_x, 1), slope_x)
    x_terms = slopes_x[3:] + along_x * slopes_x[:3]
    z_terms = whole_z_part(velocity)
    combined = 0.5 * (x_terms + z_terms)
    smoothed = solve_x(smooth_rhs(extend_x(combined), width_x, 1), smooth_x)
    return -smoothed


def per_block(velocity):
    _, rows, planes, columns = velocity.shape
    fits = planes == 1 and columns == 4 * LANES and rows % 512 == 0 and rows >= 1024
    return blocked(velocity) if fits else per_device(velocity)


def solution(mesh):
    return jax.shard_map(
        per_block,
        mesh=mesh,
        in_specs=(P(None, "gx", None, "gz"),),
        out_specs=P(None, "gx", None, "gz"),
        check_vma=False,
    )
```

```python
import functools

import numpy as np
import jax
import jax.numpy as jnp
from jax import lax
from jax.experimental import pallas as pl
from jax.experimental.pallas import tpu as pltpu
from jax.sharding import PartitionSpec as P

ALPHA_D = 1.0 / 3.0
COEF_A = 14.0 / 9.0
COEF_B = 1.0 / 9.0
ALPHA_F = 0.49
block_len = 128

LANES = 128
SUBLANES = 8
REACH_D = 24
REACH_F = 96
RIM = 128
PIECES = 8

ROOT_D = (-1.0 + np.sqrt(1.0 - 4.0 * ALPHA_D**2)) / (2.0 * ALPHA_D)
NEAR_D = COEF_B / (4.0 * ALPHA_D)
GAIN_D = (COEF_A / 2.0 - NEAR_D) * (1.0 - ROOT_D**2) / np.sqrt(1.0 - 4.0 * ALPHA_D**2)
BETA = NEAR_D / GAIN_D


def filter_coefficients():
    return (
        (11.0 + 10.0 * ALPHA_F) / 16.0,
        (15.0 + 34.0 * ALPHA_F) / 32.0,
        (-3.0 + 6.0 * ALPHA_F) / 16.0,
        (1.0 - 2.0 * ALPHA_F) / 32.0,
    )


def split_filter():
    a0, a1, a2, a3 = filter_coefficients()
    poly = [a0 - a2, 0.5 * a1 - 1.5 * a3, 0.5 * a2, 0.5 * a3]
    tap2 = poly[3] / ALPHA_F
    tap1 = (poly[2] - tap2) / ALPHA_F
    tap0 = (poly[1] - tap1) / ALPHA_F
    rest = poly[0] - tap0
    root = (-1.0 + np.sqrt(1.0 - 4.0 * ALPHA_F**2)) / (2.0 * ALPHA_F)
    gain = rest / np.sqrt(1.0 - 4.0 * ALPHA_F**2)
    return root, gain, (tap0 + 2.0 * tap2) / gain, tap1 / gain, tap2 / gain


ROOT_F, GAIN_F, TAP0, TAP1, TAP2 = (float(v) for v in split_filter())
ROOT_D, GAIN_D, BETA = float(ROOT_D), float(GAIN_D), float(BETA)
SCALE = -0.5 * GAIN_D * GAIN_F


def line_table():
    lane = np.arange(LANES)

    def kernel(offset):
        size = np.abs(offset)
        return np.sign(offset) * (ROOT_D ** (np.maximum(size, 1) - 1.0) + BETA * (size == 1))

    inside = kernel(lane[:, None] - lane[None, :])
    source = np.where(lane < LANES // 2, lane + LANES, lane - LANES)
    beside = kernel(source[:, None] - lane[None, :])
    return (SCALE * np.concatenate([inside, beside], axis=0)).astype(np.float32)


def end_table():
    lane = np.arange(LANES)
    table = np.zeros((LANES, LANES))
    tail = LANES - 2.0 - lane
    table[:, 0] = np.where((lane >= LANES // 2) & (lane < LANES - 1), ROOT_D ** np.maximum(tail, 0.0), 0.0)
    table[LANES - 1, 1] = 1.0
    table[0, 2] = 1.0
    table[:, 3] = np.where((lane < LANES // 2) & (lane > 0), ROOT_D ** np.maximum(lane - 1.0, 0.0), 0.0)
    return table.astype(np.float32)


def split_value(value):
    high = value.astype(jnp.bfloat16)
    low = (value - high.astype(jnp.float32)).astype(jnp.bfloat16)
    return high, low


def low_rows():
    return lax.broadcasted_iota(jnp.int32, (SUBLANES, LANES), 0) < SUBLANES // 2


def low_lanes(rows):
    return lax.broadcasted_iota(jnp.int32, (rows, LANES), 1) < LANES // 2


def six_fields(factor, parts):
    return list(parts) + [factor * part for part in parts]


def ends_kernel(seg, v_ref, table_ref, vel_ref, numbers_ref, table, weights, sems, sem):
    rows = LANES
    count = seg // rows

    def load(b):
        at = pl.ds(b * rows, rows)
        return [
            pltpu.make_async_copy(v_ref.at[c, h, at], vel_ref.at[c, at, pl.ds(4 * h, 4)], sems.at[b, 2 * c + h])
            for c in range(3)
            for h in range(2)
        ]

    for b in range(count):
        for copy in load(b):
            copy.start()
        if b == 0:
            fetch = pltpu.make_async_copy(table_ref, table, sem)
            fetch.start()
    fetch.wait()
    for field in range(6):
        moved = table[...] if field == 0 else pltpu.roll(table[...], 4 * field, axis=1)
        high, low = split_value(moved)
        for part in range(2):
            at = pl.ds((2 * field + part) * LANES, LANES)
            weights[at, 0:LANES] = high
            weights[at, LANES:] = low
    flat = vel_ref.reshape(3 * seg * SUBLANES, LANES)
    low_lane = low_lanes(2 * rows)

    for b in range(count):
        for copy in load(b):
            copy.wait()
        parts = []
        for c in range(3):
            chunk = []
            for n in (0, 3):
                chunk.append(
                    jnp.concatenate(
                        [
                            flat[pl.ds((c * seg + b * rows + 8 * k) * SUBLANES + 4 * h + n, 8, stride=SUBLANES), :]
                            for h in range(2)
                            for k in range(rows // 8)
                        ],
                        axis=0,
                    )
                )
            parts.append(jnp.where(low_lane, chunk[0], chunk[1]))
        pieces = []
        for field in six_fields(parts[2], parts):
            pieces += list(split_value(field))
        both = jnp.dot(jnp.concatenate(pieces, axis=1), weights[...], preferred_element_type=jnp.float32)
        numbers = both[:, :LANES] + both[:, LANES:]
        for h in range(2):
            turned = numbers[h * rows : (h + 1) * rows].T
            numbers_ref[:, pl.ds(h * seg + b * rows, rows)] = turned[0:24]


HBM = pl.BlockSpec(memory_space=pl.ANY)
VMEM = pl.BlockSpec(memory_space=pltpu.VMEM)


def ends(view, seg):
    zs = jax.ShapeDtypeStruct((24, 2 * seg), jnp.float32)
    return pl.pallas_call(
        functools.partial(ends_kernel, seg),
        out_shape=(jax.ShapeDtypeStruct((3, seg, SUBLANES, LANES), jnp.float32), zs),
        in_specs=[HBM, HBM],
        out_specs=(VMEM,) * 2,
        scratch_shapes=[
            pltpu.VMEM((LANES, LANES), jnp.float32),
            pltpu.VMEM((12 * LANES, 2 * LANES), jnp.bfloat16),
            pltpu.SemaphoreType.DMA((seg // LANES, 6)),
            pltpu.SemaphoreType.DMA,
        ],
        compiler_params=pltpu.CompilerParams(vmem_limit_bytes=44 * 2**20),
        name="line_ends",
    )(view, jnp.asarray(end_table()))


def x_kernel(seg, vel_ref, s_ref, sums_ref):
    reach = REACH_D
    first = low_rows()
    zero = jnp.zeros((SUBLANES, LANES), jnp.float32)
    start = ((zero,) * 6, (zero,) * 4)

    def advance(values, carry):
        sums, near = carry
        speed = SCALE * values[0]
        terms = six_fields(speed, values)
        bend = BETA * (near[3] + speed)
        found = [(sums[3 + c] + speed * sums[c]) + near[c] * bend for c in range(3)]
        return found, (tuple(term + ROOT_D * total for term, total in zip(terms, sums)), (*values, speed))

    def row(i):
        return [vel_ref[c, i] for c in range(3)]

    def other(i, keep_first):
        turned = [pltpu.roll(value, 4, axis=0) for value in row(i)]
        return [jnp.where(first, value, 0.0) if keep_first else jnp.where(first, 0.0, value) for value in turned]

    def forward(i, carry):
        found, carry = advance(row(i), carry)
        for c in range(3):
            s_ref[c, i] = found[c]
        return carry

    def backward(k, carry):
        i = seg - 1 - k
        found, carry = advance(row(i), carry)
        for c in range(3):
            s_ref[c, i] = found[c] - s_ref[c, i]
        return carry

    carry = lax.fori_loop(0, reach, lambda i, k: advance(other(seg - reach + i, False), k)[1], start, unroll=8)
    carry = lax.fori_loop(0, seg, forward, carry, unroll=8)
    for field in range(6):
        sums_ref[0, field] = carry[0][field]
    carry = lax.fori_loop(0, reach, lambda i, k: advance(other(reach - 1 - i, True), k)[1], start, unroll=8)
    carry = lax.fori_loop(0, seg, backward, carry, unroll=8)
    for field in range(6):
        sums_ref[1, field] = carry[0][field]


def x_part(vel, seg):
    points = 3 * 2 * seg * 4 * LANES
    return pl.pallas_call(
        functools.partial(x_kernel, seg),
        out_shape=(
            jax.ShapeDtypeStruct(vel.shape, jnp.float32),
            jax.ShapeDtypeStruct((2, 6, SUBLANES, LANES), jnp.float32),
        ),
        in_specs=[VMEM],
        out_specs=(VMEM, VMEM),
        compiler_params=pltpu.CompilerParams(vmem_limit_bytes=8 * 2**20),
        cost_estimate=pl.CostEstimate(flops=60 * points, bytes_accessed=8 * points, transcendentals=0),
        name="x_slopes",
    )(vel)


def z_kernel(
    seg, vel_ref, sx_ref, xsums_ref, table_ref, zl_ref, zr_ref,
    o_ref, rim_ref, one_ref, two_ref,
    weights, sbuf, mbuf, turn, halo_hi, halo_lo, pack, sems,
):
    far = REACH_F
    size = seg // PIECES
    step_rows = 32
    pad = step_rows
    total = seg + pad
    rows = 2 * step_rows
    first = low_rows()
    flat = vel_ref.reshape(3 * seg * SUBLANES, LANES)

    for part in range(2):
        high, low = split_value(table_ref[part * LANES : (part + 1) * LANES, :])
        for copy in range(2):
            at = pl.ds((2 * part + copy) * LANES, LANES)
            weights[at, 0:LANES] = high
            weights[at, LANES:] = low

    lane = lax.broadcasted_iota(jnp.int32, (LANES, LANES), 1)
    outer_lane = (lane >= LANES - 2) | (lane < 2)
    from_before = lax.broadcasted_iota(jnp.int32, (24, LANES), 0) % 4 < 2
    turn[24:, :] = jnp.zeros((LANES - 24, LANES), jnp.float32)
    for part in range(2 * seg // LANES):
        at = pl.ds(part * LANES, LANES)
        turn[0:24, :] = jnp.where(from_before, zl_ref[:, at], zr_ref[:, at])
        numbers = turn[...].T
        for field in range(6):
            moved = pltpu.roll(numbers, LANES - 2 - 4 * field, axis=1)
            high, low = split_value(jnp.where(outer_lane, moved, 0.0))
            halo_hi[field, at, :] = high
            halo_lo[field, at, :] = low

    low_lane = low_lanes(rows)

    def s_at(c, row):
        return pl.ds(pl.multiple_of((c * total + pad + row) * SUBLANES, SUBLANES), SUBLANES)

    def strided(c, xi, n):
        return jnp.concatenate(
            [
                flat[pl.ds((c * seg + xi + 8 * k) * SUBLANES + 4 * h + n, 8, stride=SUBLANES), :]
                for h in range(2)
                for k in range(step_rows // 8)
            ],
            axis=0,
        )

    def build(step):
        store = {}
        xi = pl.multiple_of(step * step_rows, step_rows)
        along = [[strided(c, xi, n) for c in range(3)] for n in range(4)]
        for field in range(6):
            halves = []
            for n in range(4):
                value = along[n][field % 3]
                halves.append(split_value(along[n][2] * value if field >= 3 else value))
            for which, halo in ((0, halo_hi), (1, halo_lo)):
                outer = jnp.concatenate(
                    [halo[field, pl.ds(pl.multiple_of(h * seg + xi, 16), step_rows), :] for h in range(2)], axis=0
                )
                line = [outer] + [pair[which] for pair in halves] + [outer]
                for n in range(4):
                    at = pl.ds(((field % 3 * 4 + n) * 2 + field // 3) * rows, rows)
                    store[(field % 3 * 4 + n) * 2 + field // 3, which] = line[n + 1]
                    store[(field % 3 * 4 + n) * 2 + field // 3, 2 + which] = jnp.where(low_lane, line[n + 2], line[n])
        return jnp.concatenate([jnp.concatenate([store[q, p] for p in range(4)], axis=1) for q in range(24)], axis=0)

    def finish(step, both):
        xi = pl.multiple_of(step * step_rows, step_rows)
        alongs = [strided(2, xi, n) for n in range(4)]
        for c in range(3):
            for n in range(4):
                along = alongs[n]
                base = (c * 4 + n) * 2 * rows
                plain = both[base : base + rows]
                mixed = both[base + rows : base + 2 * rows]
                term = (mixed[:, :LANES] + mixed[:, LANES:]) + along * (plain[:, :LANES] + plain[:, LANES:])
                for h in range(2):
                    for k in range(step_rows // 8):
                        at = (c * total + pad + xi + 8 * k) * SUBLANES + 4 * h + n
                        piece = h * (step_rows // 8) + k
                        sbuf[pl.ds(at, 8, stride=SUBLANES), :] = term[piece * 8 : piece * 8 + 8]

    zero = jnp.zeros((SUBLANES, LANES), jnp.float32)

    def row_of(c, row):
        return sbuf[s_at(c, row), :]

    def sweep_row(row, here, carry):
        out = []
        for c in range(3):
            down, scaled1, scaled2, one, two, three, four = carry[c]
            scaled = ROOT_F * down
            taps = TAP0 * two + TAP1 * (one + three) + TAP2 * (here[c] + four)
            mbuf[c, pad + row] = scaled2 + taps
            out.append((here[c] + scaled, scaled, scaled1, here[c], one, two, three))
        return tuple(out)

    def sweep(step, carry):
        for k in range(step_rows):
            row = step * step_rows + k
            here = []
            for c in range(3):
                here.append(row_of(c, row) + sx_ref[c, jnp.maximum(row, 0)])
                sbuf[s_at(c, row), :] = here[c]
            carry = sweep_row(row, here, carry)
        return carry

    def slopes(step):
        return jnp.dot(build(step), weights[...], preferred_element_type=jnp.float32)

    steps = seg // step_rows
    for c in range(3):
        sbuf[pl.ds(c * total * SUBLANES, pad * SUBLANES), :] = jnp.zeros((pad * SUBLANES, LANES), jnp.float32)
    fresh = ((zero,) * 7,) * 3

    def block(pair, carry):
        both = slopes(2 * pair)
        carry = sweep(2 * pair - 1, carry)
        carry = jax.tree.map(lambda value: jnp.where(pair > 0, value, 0.0), carry)
        finish(2 * pair, both)
        both = slopes(2 * pair + 1)
        carry = sweep(2 * pair, carry)
        finish(2 * pair + 1, both)
        return carry

    carry = lax.fori_loop(0, steps // 2, block, fresh)
    carry = sweep(steps - 1, carry)
    down = [carry[c][0] for c in range(3)]
    for k in range(2):
        carry = sweep_row(seg + k, (zero,) * 3, carry)

    low_end = [[pltpu.roll(row_of(c, seg - 1 - k), 4, axis=0) for k in range(2)] for c in range(3)]
    high_start = [[pltpu.roll(row_of(c, k), 4, axis=0) for k in range(2)] for c in range(3)]
    inward = [jnp.where(first, 0.0, pltpu.roll(value, 4, axis=0)) for value in down]

    def carry_over(k, carry):
        out = []
        for c in range(3):
            value = ROOT_F * carry[c]
            mbuf[c, pad + 2 + k] = mbuf[c, pad + 2 + k] + value
            out.append(value)
        return tuple(out)

    lax.fori_loop(0, far, carry_over, tuple(inward), unroll=8)
    for c in range(3):
        begin, end = low_end[c], high_start[c]
        for k, add in ((0, TAP1 * begin[0] + TAP2 * begin[1]), (1, TAP2 * begin[0])):
            mbuf[c, pad + 2 + k] = mbuf[c, pad + 2 + k] + jnp.where(first, 0.0, add)
        for k, add in ((seg - 1, TAP1 * end[0] + TAP2 * end[1]), (seg - 2, TAP2 * end[0])):
            mbuf[c, pad + 2 + k] = mbuf[c, pad + 2 + k] + jnp.where(first, add, 0.0)

    def warm(k, sums):
        return tuple(
            jnp.where(first, pltpu.roll(row_of(c, far - 1 - k), 4, axis=0), 0.0) + ROOT_F * sums[c] for c in range(3)
        )

    sums = lax.fori_loop(0, far, warm, (zero,) * 3, unroll=8)

    def backward(b):
        def body(i, sums):
            row = b * size + size - 1 - i
            out = []
            for c in range(3):
                up = row_of(c, row) + ROOT_F * sums[c]
                mbuf[c, pad + 2 + row] = up + mbuf[c, pad + 2 + row]
                out.append(up)
            return tuple(out)

        return body

    def store(b):
        at = pl.ds(b * size, size)
        held = pl.ds(pad + 2 + b * size, size)
        edge = RIM // size
        return [
            pltpu.make_async_copy(mbuf.at[c, held, pl.ds(4 * h, 4)], o_ref.at[c, h, at], sems.at[b, 2 * c + h])
            for c in range(3)
            for h in range(2)
            if (b >= edge if h == 0 else b < PIECES - edge)
        ]

    for b in reversed(range(PIECES)):
        sums = lax.fori_loop(0, size, backward(b), sums, unroll=16)
        for copy in store(b):
            copy.start()

    def to_rim(k, _):
        for c in range(3):
            rim_ref[c, k] = jnp.where(first, mbuf[c, pad + 2 + k], mbuf[c, pad + 1 + seg - k])
        return 0

    lax.fori_loop(0, RIM, to_rim, 0, unroll=8)

    for field in range(6):
        pack[field] = jnp.where(first, xsums_ref[1, field], xsums_ref[0, field])
    for c in range(3):
        pack[6 + c] = jnp.where(first, vel_ref[c, 0], vel_ref[c, seg - 1])
        pack[9 + c] = jnp.where(first, sums[c], down[c])
        pack[12 + c] = jnp.where(first, row_of(c, 0), row_of(c, seg - 1))
        pack[15 + c] = jnp.where(first, row_of(c, 1), row_of(c, seg - 2))
    weighted = zero
    for k in reversed(range(REACH_D)):
        weighted = jnp.where(first, vel_ref[0, k], vel_ref[0, seg - 1 - k]) + (ROOT_F * ROOT_D) * weighted
    pack[18] = SCALE * weighted
    pack[19] = SCALE * jnp.where(first, vel_ref[0, 1], vel_ref[0, seg - 2])
    even = lax.axis_index("gx") % 2 == 0
    one_ref[...] = jnp.where(even, pack[:, 4:8, :], pack[:, 0:4, :])
    two_ref[...] = jnp.where(even, pack[:, 0:4, :], pack[:, 4:8, :])
    for b in reversed(range(PIECES)):
        for copy in store(b):
            copy.wait()


def z_part(vel, local, xsums, seg, before_z, after_z):
    side = jax.ShapeDtypeStruct((20, 4, LANES), jnp.float32)
    pad = 32
    return pl.pallas_call(
        functools.partial(z_kernel, seg),
        out_shape=(
            jax.ShapeDtypeStruct((3, 2, seg, 4, LANES), jnp.float32),
            jax.ShapeDtypeStruct((3, RIM, SUBLANES, LANES), jnp.float32),
            side,
            side,
        ),
        in_specs=[VMEM] * 6,
        out_specs=(HBM, VMEM, VMEM, VMEM),
        scratch_shapes=[
            pltpu.VMEM((4 * LANES, 2 * LANES), jnp.bfloat16),
            pltpu.VMEM((3 * (seg + pad) * SUBLANES, LANES), jnp.float32),
            pltpu.VMEM((3, seg + pad + 2, SUBLANES, LANES), jnp.float32),
            pltpu.VMEM((LANES, LANES), jnp.float32),
            pltpu.VMEM((6, 2 * seg, LANES), jnp.bfloat16),
            pltpu.VMEM((6, 2 * seg, LANES), jnp.bfloat16),
            pltpu.VMEM((20, SUBLANES, LANES), jnp.float32),
            pltpu.SemaphoreType.DMA((PIECES, 6)),
        ],
        compiler_params=pltpu.CompilerParams(vmem_limit_bytes=32 * 2**20),
        name="z_slopes_and_filter",
    )(vel, local, xsums, jnp.asarray(line_table()), before_z, after_z)


def rim_kernel(seg, o_in, rim_ref, vel_ref, xsums_ref, one_ref, two_ref, o_ref, edge, top, bottom, sems):
    del o_in
    reach = REACH_D
    first = low_rows()
    sign = jnp.where(first, -1.0, 1.0).astype(jnp.float32)
    even = lax.axis_index("gx") % 2 == 0
    edge[:, 0:4, :] = jnp.where(even, two_ref[...], one_ref[...])
    edge[:, 4:8, :] = jnp.where(even, one_ref[...], two_ref[...])
    own = [jnp.where(first, xsums_ref[1, field], xsums_ref[0, field]) for field in range(6)]
    raw = [jnp.where(first, vel_ref[c, 0], vel_ref[c, seg - 1]) for c in range(3)]
    speeds = [SCALE * jnp.where(first, vel_ref[0, k], vel_ref[0, seg - 1 - k]) for k in range(reach)]
    next_to, second = SCALE * edge[6], edge[19]
    for c in range(3):
        bend = (BETA * raw[c]) * (speeds[0] + next_to)
        close = edge[12 + c] - sign * ((own[3 + c] + next_to * own[c]) + bend)
        further = edge[15 + c] - sign * (ROOT_D * (own[3 + c] + second * own[c]))
        gain = 1.0 / (1.0 - ROOT_F * ROOT_D)
        total = edge[9 + c] - sign * ((gain * own[3 + c] + edge[18] * own[c]) + bend)
        change = [
            (sign * ROOT_D**k) * (edge[3 + c] + speeds[k] * edge[c]) for k in range(reach)
        ]
        change[0] = change[0] + sign * ((BETA * edge[6 + c]) * (next_to + speeds[0]))
        line = [further, close] + change + [jnp.zeros_like(close)] * 4
        ups = [None] * reach
        up = jnp.zeros_like(close)
        for k in reversed(range(reach)):
            up = change[k] + ROOT_F * up
            ups[k] = up
        for k in range(RIM):
            scaled = ROOT_F * total
            found = scaled
            if k < reach + 2:
                here = line[k + 2]
                taps = TAP0 * here + TAP1 * (line[k + 1] + line[k + 3]) + TAP2 * (line[k] + line[k + 4])
                found = found + taps
            if k < reach:
                found = found + ups[k]
                total = change[k] + scaled
            else:
                total = scaled
            fixed = rim_ref[c, k] + found
            top[c, k] = fixed
            bottom[c, RIM - 1 - k] = fixed
        pltpu.make_async_copy(top.at[c, :, pl.ds(0, 4)], o_ref.at[c, 0, pl.ds(0, RIM)], sems.at[c, 0]).start()
        pltpu.make_async_copy(
            bottom.at[c, :, pl.ds(4, 4)], o_ref.at[c, 1, pl.ds(seg - RIM, RIM)], sems.at[c, 1]
        ).start()
    for c in range(3):
        pltpu.make_async_copy(top.at[c, :, pl.ds(0, 4)], o_ref.at[c, 0, pl.ds(0, RIM)], sems.at[c, 0]).wait()
        pltpu.make_async_copy(
            bottom.at[c, :, pl.ds(4, 4)], o_ref.at[c, 1, pl.ds(seg - RIM, RIM)], sems.at[c, 1]
        ).wait()


def rim_part(out, rim, vel, xsums, one, two, seg):
    return pl.pallas_call(
        functools.partial(rim_kernel, seg),
        out_shape=jax.ShapeDtypeStruct(out.shape, jnp.float32),
        in_specs=[HBM] + [VMEM] * 5,
        out_specs=HBM,
        input_output_aliases={0: 0},
        scratch_shapes=[
            pltpu.VMEM((20, SUBLANES, LANES), jnp.float32),
            pltpu.VMEM((3, RIM, SUBLANES, LANES), jnp.float32),
            pltpu.VMEM((3, RIM, SUBLANES, LANES), jnp.float32),
            pltpu.SemaphoreType.DMA((3, 2)),
        ],
        compiler_params=pltpu.CompilerParams(vmem_limit_bytes=16 * 2**20),
        name="rim",
    )(out, rim, vel, xsums, one, two)


def ring(axis):
    count = lax.axis_size(axis)
    forward = [(i, (i + 1) % count) for i in range(count)]
    return forward, [(target, source) for source, target in forward]


def pairs(axis):
    count = lax.axis_size(axis)
    one = [(i, i + 1 if i % 2 == 0 else i - 1) for i in range(count)]
    two = [(i, (i - 1 if i % 2 == 0 else i + 1) % count) for i in range(count)]
    return one, two


def blocked(velocity):
    seg = velocity.shape[1] // 2
    vel, numbers = ends(velocity.reshape(3, 2, seg, 4, LANES), seg)
    forward, backward = ring("gz")
    before_z = lax.ppermute(numbers, "gz", forward)
    after_z = lax.ppermute(numbers, "gz", backward)
    local, xsums = x_part(vel, seg)
    out, rim, one, two = z_part(vel, local, xsums, seg, before_z, after_z)
    first_swap, second_swap = pairs("gx")
    one = lax.ppermute(one, "gx", first_swap)
    two = lax.ppermute(two, "gx", second_swap)
    return rim_part(out, rim, vel, xsums, one, two, seg).reshape(velocity.shape)


def with_halo(block, sides, width):
    for axis, dim in sides:
        count = lax.axis_size(axis)
        forward = [(i, i + 1) for i in range(count - 1)]
        forward.append((count - 1, 0))
        backward = [(target, source) for source, target in forward]
        low = lax.ppermute(
            lax.slice_in_dim(block, block.shape[dim] - width, None, axis=dim), axis, forward
        )
        high = lax.ppermute(lax.slice_in_dim(block, 0, width, axis=dim), axis, backward)
        block = jnp.concatenate([low, block, high], axis=dim)
    return block


def tables(length, alpha):
    lower_diag = jnp.concatenate(
        [jnp.zeros((1,), jnp.float32), jnp.full((length - 1,), alpha, jnp.float32)]
    )
    upper_diag = jnp.concatenate(
        [jnp.full((length - 1,), alpha, jnp.float32), jnp.zeros((1,), jnp.float32)]
    )
    main_diag = jnp.ones((length,), jnp.float32)
    identity = jnp.eye(length, dtype=jnp.float32)
    inverse = lax.linalg.tridiagonal_solve(lower_diag, main_diag, upper_diag, identity)
    left_col = alpha * inverse[:, 0]
    right_col = alpha * inverse[:, length - 1]
    coupling = alpha * inverse[0, 0]
    return (inverse, left_col, right_col, coupling)


def offset_slice(extended, offset, length, direction, base=3):
    return lax.slice_in_dim(extended, base + offset, base + offset + length, axis=direction)


def slope_rhs(extended, length, direction, base=3):
    rhs = (
        COEF_A
        * 0.5
        * (
            offset_slice(extended, 1, length, direction, base)
            - offset_slice(extended, -1, length, direction, base)
        )
    )
    return rhs + COEF_B * 0.25 * (
        offset_slice(extended, 2, length, direction, base)
        - offset_slice(extended, -2, length, direction, base)
    )


def smooth_rhs(extended, length, direction, base=3):
    coefficients = filter_coefficients()
    rhs = coefficients[0] * offset_slice(extended, 0, length, direction, base)
    for offset in range(1, 4):
        rhs = rhs + 0.5 * coefficients[offset] * (
            offset_slice(extended, offset, length, direction, base)
            + offset_slice(extended, -offset, length, direction, base)
        )
    return rhs


def wrap_pad(values, direction):
    length = values.shape[direction]
    return jnp.concatenate(
        [
            lax.slice_in_dim(values, length - 3, length, axis=direction),
            values,
            lax.slice_in_dim(values, 0, 3, axis=direction),
        ],
        axis=direction,
    )


def apply_along(inverse, values, direction):
    rotated = jnp.tensordot(
        inverse, values, axes=([1], [direction]), precision=lax.Precision.HIGHEST
    )
    return jnp.moveaxis(rotated, 0, direction)


def end_values(partial_value, direction):
    length = partial_value.shape[direction]
    first_val = lax.slice_in_dim(partial_value, 0, 1, axis=direction)
    last_val = lax.slice_in_dim(partial_value, length - 1, length, axis=direction)
    return (first_val, last_val)


def corrected(partial_value, prev_last, next_first, table, direction):
    inverse, left_col, right_col, coupling = table
    first_val, last_val = end_values(partial_value, direction)
    factor_inv = 1.0 / (1.0 - coupling * coupling)
    left_value = (prev_last - coupling * first_val) * factor_inv
    right_value = (next_first - coupling * last_val) * factor_inv
    dims_list = [1] * partial_value.ndim
    dims_list[direction] = partial_value.shape[direction]
    return (
        partial_value
        - left_col.reshape(dims_list) * left_value
        - right_col.reshape(dims_list) * right_value
    )


def extend_x(values):
    return with_halo(values, (("gx", 1),), 3)


def solve_x(rhs, table):
    partial_value = apply_along(table[0], rhs, 1)
    first_val, last_val = end_values(partial_value, 1)
    beside = with_halo(jnp.concatenate([first_val, last_val], axis=1), (("gx", 1),), 1)
    return corrected(partial_value, beside[:, 0:1], beside[:, 3:4], table, 1)


def solve_blocks(rhs, table):
    dims_list = rhs.shape
    blocks = rhs.reshape(dims_list[:-1] + (dims_list[-1] // block_len, block_len))
    last_dim = blocks.ndim - 1
    partial_value = apply_along(table[0], blocks, last_dim)
    first_val, last_val = end_values(partial_value, last_dim)
    prev_last = jnp.roll(last_val, 1, axis=last_dim - 1)
    next_first = jnp.roll(first_val, -1, axis=last_dim - 1)
    return corrected(partial_value, prev_last, next_first, table, last_dim).reshape(dims_list)


def whole_z_part(velocity):
    slope_z = tables(block_len, ALPHA_D)
    pencil = lax.all_to_all(velocity, "gz", split_axis=1, concat_axis=3, tiled=True)
    along_z = pencil[2:3]
    fields = jnp.concatenate([pencil, along_z * pencil], axis=0)
    slopes = solve_blocks(slope_rhs(wrap_pad(fields, 3), fields.shape[3], 3), slope_z)
    local_terms = slopes[3:] + along_z * slopes[:3]
    return lax.all_to_all(local_terms, "gz", split_axis=3, concat_axis=1, tiled=True)


def per_device(velocity):
    width_x = velocity.shape[1]
    slope_x = tables(width_x, ALPHA_D)
    smooth_x = tables(width_x, ALPHA_F)
    along_x = velocity[0:1]
    rim_source = jnp.concatenate([velocity, along_x * velocity], axis=0)
    padded = extend_x(rim_source)
    slopes_x = solve_x(slope_rhs(padded, width_x, 1), slope_x)
    x_terms = slopes_x[3:] + along_x * slopes_x[:3]
    z_terms = whole_z_part(velocity)
    combined = 0.5 * (x_terms + z_terms)
    smoothed = solve_x(smooth_rhs(extend_x(combined), width_x, 1), smooth_x)
    return -smoothed


def per_block(velocity):
    _, rows, planes, columns = velocity.shape
    fits = planes == 1 and columns == 4 * LANES and rows % 1024 == 0 and lax.axis_size("gx") % 2 == 0
    return blocked(velocity) if fits else per_device(velocity)


def solution(mesh):
    return jax.shard_map(
        per_block,
        mesh=mesh,
        in_specs=(P(None, "gx", None, "gz"),),
        out_specs=P(None, "gx", None, "gz"),
        check_vma=False,
    )
```

```python
import functools

import numpy as np
import jax
import jax.numpy as jnp
from jax import lax
from jax.experimental import pallas as pl
from jax.experimental.pallas import tpu as pltpu
from jax.sharding import PartitionSpec as P

ALPHA_D = 1.0 / 3.0
COEF_A = 14.0 / 9.0
COEF_B = 1.0 / 9.0
ALPHA_F = 0.49
block_len = 128

LANES = 128
SUBLANES = 8
REACH_D = 24
REACH_F = 96
RIM = 128
STEP_ROWS = 64
PIECES = 4
AHEAD = 4
GROUP = 4

ROOT_D = (-1.0 + np.sqrt(1.0 - 4.0 * ALPHA_D**2)) / (2.0 * ALPHA_D)
NEAR_D = COEF_B / (4.0 * ALPHA_D)
GAIN_D = (COEF_A / 2.0 - NEAR_D) * (1.0 - ROOT_D**2) / np.sqrt(1.0 - 4.0 * ALPHA_D**2)
BETA = NEAR_D / GAIN_D


def filter_coefficients():
    return (
        (11.0 + 10.0 * ALPHA_F) / 16.0,
        (15.0 + 34.0 * ALPHA_F) / 32.0,
        (-3.0 + 6.0 * ALPHA_F) / 16.0,
        (1.0 - 2.0 * ALPHA_F) / 32.0,
    )


def split_filter():
    a0, a1, a2, a3 = filter_coefficients()
    poly = [a0 - a2, 0.5 * a1 - 1.5 * a3, 0.5 * a2, 0.5 * a3]
    tap2 = poly[3] / ALPHA_F
    tap1 = (poly[2] - tap2) / ALPHA_F
    tap0 = (poly[1] - tap1) / ALPHA_F
    rest = poly[0] - tap0
    root = (-1.0 + np.sqrt(1.0 - 4.0 * ALPHA_F**2)) / (2.0 * ALPHA_F)
    gain = rest / np.sqrt(1.0 - 4.0 * ALPHA_F**2)
    return root, gain, (tap0 + 2.0 * tap2) / gain, tap1 / gain, tap2 / gain


ROOT_F, GAIN_F, TAP0, TAP1, TAP2 = (float(v) for v in split_filter())
ROOT_D, GAIN_D, BETA = float(ROOT_D), float(GAIN_D), float(BETA)
SCALE = -0.5 * GAIN_D * GAIN_F


def line_table():
    lane = np.arange(LANES)

    def kernel(offset):
        size = np.abs(offset)
        return np.sign(offset) * (ROOT_D ** (np.maximum(size, 1) - 1.0) + BETA * (size == 1))

    inside = kernel(lane[:, None] - lane[None, :])
    source = np.where(lane < LANES // 2, lane + LANES, lane - LANES)
    beside = kernel(source[:, None] - lane[None, :])
    return (SCALE * np.concatenate([inside, beside], axis=0)).astype(np.float32)


def end_table():
    row = lax.broadcasted_iota(jnp.int32, (LANES, LANES), 0)
    lane = lax.broadcasted_iota(jnp.int32, (LANES, LANES), 1)
    starts = row < LANES // 2
    steps = jnp.where(starts, row - 1, LANES - 2 - row)
    size = jnp.exp(float(np.log(-ROOT_D)) * jnp.maximum(steps, 0).astype(jnp.float32))
    power = jnp.where(steps % 2 == 0, size, -size)
    inner = (steps >= 0) & (lane == jnp.where(starts, 3, 0))
    edge = (steps < 0) & (lane == jnp.where(starts, 2, 1))
    return jnp.where(inner, power, jnp.where(edge, 1.0, 0.0))


def split_value(value):
    high = value.astype(jnp.bfloat16)
    low = (value - high.astype(jnp.float32)).astype(jnp.bfloat16)
    return high, low


def low_rows():
    return lax.broadcasted_iota(jnp.int32, (SUBLANES, LANES), 0) < SUBLANES // 2


def low_lanes(rows):
    return lax.broadcasted_iota(jnp.int32, (rows, LANES), 1) < LANES // 2


def six_fields(factor, parts):
    return list(parts) + [factor * part for part in parts]


def ends_kernel(seg, v_ref, vel_ref, numbers_ref, weights, sems):
    rows = LANES
    count = seg // rows

    def load(b):
        at = pl.ds(b * rows, rows)
        return [
            pltpu.make_async_copy(v_ref.at[c, h, at], vel_ref.at[c, at, pl.ds(4 * h, 4)], sems.at[b, 2 * c + h])
            for c in range(3)
            for h in range(2)
        ]

    for b in range(AHEAD):
        for copy in load(b):
            copy.start()
    table = end_table()
    for field in range(6):
        moved = table if field == 0 else pltpu.roll(table, 4 * field, axis=1)
        high, low = split_value(moved)
        for part in range(2):
            at = pl.ds((2 * field + part) * LANES, LANES)
            weights[at, 0:LANES] = high
            weights[at, LANES:] = low
    low_lane = low_lanes(2 * rows)
    flat = vel_ref.reshape(3 * seg * SUBLANES, LANES)

    for b in range(count):
        for copy in load(b):
            copy.wait()
        if b + AHEAD < count:
            for copy in load(b + AHEAD):
                copy.start()
        parts = []
        for c in range(3):
            start, end = (
                jnp.concatenate(
                    [
                        flat[pl.ds((c * seg + b * rows + 8 * k) * SUBLANES + 4 * h + n, 8, stride=SUBLANES), :]
                        for h in range(2)
                        for k in range(rows // 8)
                    ],
                    axis=0,
                )
                for n in (0, 3)
            )
            parts.append(jnp.where(low_lane, start, end))
        pieces = []
        for field in six_fields(parts[2], parts):
            pieces += list(split_value(field))
        both = jnp.dot(jnp.concatenate(pieces, axis=1), weights[...], preferred_element_type=jnp.float32)
        numbers = both[:, :LANES] + both[:, LANES:]
        for h in range(2):
            turned = numbers[h * rows : (h + 1) * rows].T
            numbers_ref[:, pl.ds(h * seg + b * rows, rows)] = turned[0:24]


HBM = pl.BlockSpec(memory_space=pl.ANY)
VMEM = pl.BlockSpec(memory_space=pltpu.VMEM)


def ends(view, seg):
    return pl.pallas_call(
        functools.partial(ends_kernel, seg),
        out_shape=(
            jax.ShapeDtypeStruct((3, seg, SUBLANES, LANES), jnp.float32),
            jax.ShapeDtypeStruct((24, 2 * seg), jnp.float32),
        ),
        in_specs=[HBM],
        out_specs=(VMEM, VMEM),
        scratch_shapes=[
            pltpu.VMEM((12 * LANES, 2 * LANES), jnp.bfloat16),
            pltpu.SemaphoreType.DMA((seg // LANES, 6)),
        ],
        compiler_params=pltpu.CompilerParams(vmem_limit_bytes=44 * 2**20),
        name="line_ends",
    )(view)


def x_kernel(seg, vel_ref, s_ref, sums_ref):
    reach = REACH_D
    first = low_rows()
    zero = jnp.zeros((SUBLANES, LANES), jnp.float32)
    start = ((zero,) * 6, (zero,) * 4)

    def advance(values, carry):
        sums, near = carry
        speed = SCALE * values[0]
        terms = six_fields(speed, values)
        bend = BETA * (near[3] + speed)
        found = [(sums[3 + c] + speed * sums[c]) + near[c] * bend for c in range(3)]
        return found, (tuple(term + ROOT_D * total for term, total in zip(terms, sums)), (*values, speed))

    def row(i):
        return [vel_ref[c, i] for c in range(3)]

    def other(i, keep_first):
        turned = [pltpu.roll(value, 4, axis=0) for value in row(i)]
        return [jnp.where(first, value, 0.0) if keep_first else jnp.where(first, 0.0, value) for value in turned]

    def forward(i, carry):
        found, carry = advance(row(i), carry)
        for c in range(3):
            s_ref[c, i] = found[c]
        return carry

    def backward(k, carry):
        i = seg - 1 - k
        found, carry = advance(row(i), carry)
        for c in range(3):
            s_ref[c, i] = found[c] - s_ref[c, i]
        return carry

    carry = lax.fori_loop(0, reach, lambda i, k: advance(other(seg - reach + i, False), k)[1], start, unroll=8)
    carry = lax.fori_loop(0, seg, forward, carry, unroll=16)
    for field in range(6):
        sums_ref[0, field] = carry[0][field]
    carry = lax.fori_loop(0, reach, lambda i, k: advance(other(reach - 1 - i, True), k)[1], start, unroll=8)
    carry = lax.fori_loop(0, seg, backward, carry, unroll=16)
    for field in range(6):
        sums_ref[1, field] = carry[0][field]


def x_part(vel, seg):
    points = 3 * 2 * seg * 4 * LANES
    return pl.pallas_call(
        functools.partial(x_kernel, seg),
        out_shape=(
            jax.ShapeDtypeStruct(vel.shape, jnp.float32),
            jax.ShapeDtypeStruct((2, 6, SUBLANES, LANES), jnp.float32),
        ),
        in_specs=[VMEM],
        out_specs=(VMEM, VMEM),
        compiler_params=pltpu.CompilerParams(vmem_limit_bytes=16 * 2**20),
        cost_estimate=pl.CostEstimate(flops=60 * points, bytes_accessed=8 * points, transcendentals=0),
        name="x_slopes",
    )(vel)


def z_kernel(
    seg, vel_ref, sx_ref, xsums_ref, table_ref, zl_ref, zr_ref,
    sbuf, ups_ref, downs_ref, one_ref, two_ref,
    weights, turn, halo_hi, halo_lo, pack,
):
    far = REACH_F
    step_rows = STEP_ROWS
    rows = 2 * step_rows
    first = low_rows()
    flat = vel_ref.reshape(3 * seg * SUBLANES, LANES)

    for part in range(2):
        high, low = split_value(table_ref[part * LANES : (part + 1) * LANES, :])
        for copy in range(2):
            at = pl.ds((2 * part + copy) * LANES, LANES)
            weights[at, 0:LANES] = high
            weights[at, LANES:] = low

    lane = lax.broadcasted_iota(jnp.int32, (LANES, LANES), 1)
    outer_lane = (lane >= LANES - 2) | (lane < 2)
    from_before = lax.broadcasted_iota(jnp.int32, (24, LANES), 0) % 4 < 2
    turn[24:, :] = jnp.zeros((LANES - 24, LANES), jnp.float32)
    for part in range(2 * seg // LANES):
        at = pl.ds(part * LANES, LANES)
        turn[0:24, :] = jnp.where(from_before, zl_ref[:, at], zr_ref[:, at])
        numbers = turn[...].T
        for field in range(6):
            moved = pltpu.roll(numbers, LANES - 2 - 4 * field, axis=1)
            high, low = split_value(jnp.where(outer_lane, moved, 0.0))
            halo_hi[field, at, :] = high
            halo_lo[field, at, :] = low

    low_lane = jnp.where(low_lanes(rows), 1.0, 0.0).astype(jnp.bfloat16) > 0.5

    def strided(c, xi, n):
        return jnp.concatenate(
            [
                flat[pl.ds((c * seg + xi + 8 * k) * SUBLANES + 4 * h + n, 8, stride=SUBLANES), :]
                for h in range(2)
                for k in range(step_rows // 8)
            ],
            axis=0,
        )

    def build(step):
        store = {}
        xi = pl.multiple_of(step * step_rows, step_rows)
        along = [[strided(c, xi, n) for c in range(3)] for n in range(4)]
        for field in range(6):
            halves = []
            for n in range(4):
                value = along[n][field % 3]
                halves.append(split_value(along[n][2] * value if field >= 3 else value))
            for which, halo in ((0, halo_hi), (1, halo_lo)):
                outer = jnp.concatenate(
                    [halo[field, pl.ds(pl.multiple_of(h * seg + xi, 16), step_rows), :] for h in range(2)], axis=0
                )
                line = [outer] + [pair[which] for pair in halves] + [outer]
                for n in range(4):
                    at = pl.ds(((field % 3 * 4 + n) * 2 + field // 3) * rows, rows)
                    store[(field % 3 * 4 + n) * 2 + field // 3, which] = line[n + 1]
                    store[(field % 3 * 4 + n) * 2 + field // 3, 2 + which] = jnp.where(low_lane, line[n + 2], line[n])
        return jnp.concatenate([jnp.concatenate([store[q, p] for p in range(4)], axis=1) for q in range(24)], axis=0)

    def finish(step, both):
        xi = pl.multiple_of(step * step_rows, step_rows)
        alongs = [strided(2, xi, n) for n in range(4)]
        for c in range(3):
            for n in range(4):
                along = alongs[n]
                base = (c * 4 + n) * 2 * rows
                plain = both[base : base + rows]
                mixed = both[base + rows : base + 2 * rows]
                term = (mixed[:, :LANES] + mixed[:, LANES:]) + along * (plain[:, :LANES] + plain[:, LANES:])
                for h in range(2):
                    for k in range(step_rows // 8):
                        at = (c * seg + xi + 8 * k) * SUBLANES + 4 * h + n
                        piece = h * (step_rows // 8) + k
                        sbuf[pl.ds(at, 8, stride=SUBLANES), :] = term[piece * 8 : piece * 8 + 8]

    zero = jnp.zeros((SUBLANES, LANES), jnp.float32)

    def block(step, _):
        finish(step, jnp.dot(build(step), weights[...], preferred_element_type=jnp.float32))
        return 0

    lax.fori_loop(0, seg // step_rows, block, 0)

    def row_of(c, row):
        at = pl.ds(pl.multiple_of((c * seg + row) * SUBLANES, SUBLANES), SUBLANES)
        return sbuf[at, :] + sx_ref[c, row]

    def sums_of(k, sums):
        ups, downs = sums
        ups = tuple(row_of(c, far - 1 - k) + ROOT_F * ups[c] for c in range(3))
        downs = tuple(row_of(c, seg - far + k) + ROOT_F * downs[c] for c in range(3))
        return ups, downs

    ups, downs = lax.fori_loop(0, far, sums_of, ((zero,) * 3,) * 2, unroll=8)
    for c in range(3):
        ups_ref[c] = ups[c]
        downs_ref[c] = downs[c]

    for field in range(6):
        pack[field] = jnp.where(first, xsums_ref[1, field], xsums_ref[0, field])
    for c in range(3):
        pack[6 + c] = jnp.where(first, vel_ref[c, 0], vel_ref[c, seg - 1])
        pack[9 + c] = jnp.where(first, ups[c], downs[c])
        pack[12 + c] = jnp.where(first, row_of(c, 0), row_of(c, seg - 1))
        pack[15 + c] = jnp.where(first, row_of(c, 1), row_of(c, seg - 2))
    weighted = zero
    for k in reversed(range(REACH_D)):
        weighted = jnp.where(first, vel_ref[0, k], vel_ref[0, seg - 1 - k]) + (ROOT_F * ROOT_D) * weighted
    pack[18] = SCALE * weighted
    pack[19] = SCALE * jnp.where(first, vel_ref[0, 1], vel_ref[0, seg - 2])
    even = lax.axis_index("gx") % 2 == 0
    one_ref[...] = jnp.where(even, pack[:, 4:8, :], pack[:, 0:4, :])
    two_ref[...] = jnp.where(even, pack[:, 0:4, :], pack[:, 4:8, :])


def z_part(vel, local, xsums, seg, before_z, after_z):
    side = jax.ShapeDtypeStruct((20, 4, LANES), jnp.float32)
    return pl.pallas_call(
        functools.partial(z_kernel, seg),
        out_shape=(
            jax.ShapeDtypeStruct((3 * seg * SUBLANES, LANES), jnp.float32),
            jax.ShapeDtypeStruct((3, SUBLANES, LANES), jnp.float32),
            jax.ShapeDtypeStruct((3, SUBLANES, LANES), jnp.float32),
            side,
            side,
        ),
        in_specs=[VMEM] * 6,
        out_specs=(VMEM,) * 5,
        scratch_shapes=[
            pltpu.VMEM((4 * LANES, 2 * LANES), jnp.bfloat16),
            pltpu.VMEM((LANES, LANES), jnp.float32),
            pltpu.VMEM((6, 2 * seg, LANES), jnp.bfloat16),
            pltpu.VMEM((6, 2 * seg, LANES), jnp.bfloat16),
            pltpu.VMEM((20, SUBLANES, LANES), jnp.float32),
        ],
        compiler_params=pltpu.CompilerParams(vmem_limit_bytes=20 * 2**20),
        name="z_slopes",
    )(vel, local, xsums, jnp.asarray(line_table()), before_z, after_z)


def filter_kernel(seg, z_ref, x_ref, ups_ref, downs_ref, o_ref, rim_ref, s_buf, o_buf, sems):
    size = seg // PIECES
    turns = size // GROUP
    warm_group = REACH_F // turns
    first = low_rows()

    def term(c, row):
        at = pl.ds(pl.multiple_of((c * seg + row) * SUBLANES, SUBLANES), SUBLANES)
        return z_ref[at, :] + x_ref[c, row]

    def to_second(value):
        return jnp.where(first, 0.0, pltpu.roll(value, 4, axis=0))

    def to_first(value):
        return jnp.where(first, pltpu.roll(value, 4, axis=0), 0.0)

    def down_row(here, carry):
        found, out = [], []
        for c in range(3):
            down, scaled1, scaled2, one, two, three, four = carry[c]
            scaled = ROOT_F * down
            taps = TAP0 * two + TAP1 * (one + three) + TAP2 * (here[c] + four)
            found.append(scaled2 + taps)
            out.append((here[c] + scaled, scaled, scaled1, here[c], one, two, three))
        return found, tuple(out)

    def down_rows(b, i, carry):
        low = b * size + 2 + GROUP * i
        count = GROUP
        lines = [[term(c, low + k) for c in range(3)] for k in range(count)]
        results = []
        for here in lines:
            found, carry = down_row(here, carry)
            results.append(found)
        for k in range(count):
            for c in range(3):
                s_buf[c, low + k] = lines[k][c]
                o_buf[c, low + k - 2] = results[k][c]
        return carry

    def warm_rows(b, i, ups):
        top = (b + 1) * size + REACH_F - 1 - warm_group * i
        lines = [[term(c, top - k) for c in range(3)] for k in range(warm_group)]
        for here in lines:
            ups = tuple(here[c] + ROOT_F * ups[c] for c in range(3))
        return ups

    def up_rows(b, i, ups):
        low = (b + 1) * size - GROUP * (i + 1)
        order = list(reversed(range(GROUP)))
        here = {(k, c): s_buf[c, low + k] for k in order for c in range(3)}
        found = {(k, c): o_buf[c, low + k] for k in order for c in range(3)}
        for k in order:
            ups = tuple(here[k, c] + ROOT_F * ups[c] for c in range(3))
            for c in range(3):
                found[k, c] = found[k, c] + ups[c]
        for k in order:
            for c in range(3):
                o_buf[c, low + k] = found[k, c]
        return ups

    def store(b):
        at = pl.ds(b * size, size)
        edge = RIM // size
        return [
            pltpu.make_async_copy(o_buf.at[c, at, pl.ds(4 * h, 4)], o_ref.at[c, h, at], sems.at[b, 2 * c + h])
            for c in range(3)
            for h in range(2)
            if (b >= edge if h == 0 else b < PIECES - edge)
        ]

    zero = jnp.zeros((SUBLANES, LANES), jnp.float32)
    zeros = (zero,) * 3
    carry = tuple(
        (
            to_second(downs_ref[c]), zero, zero,
            to_second(term(c, seg - 1)), to_second(term(c, seg - 2)), zero, zero,
        )
        for c in range(3)
    )
    for k in range(2):
        here = [term(c, k) for c in range(3)]
        for c in range(3):
            s_buf[c, k] = here[c]
        carry = down_row(here, carry)[1]
    for c in range(3):
        for k in range(2):
            s_buf[c, seg + k] = to_first(s_buf[c, k])
    last = tuple(to_first(ups_ref[c]) for c in range(3))

    def opening(i, state):
        carry, warmed = state
        return down_rows(0, i, carry), warm_rows(0, i, warmed)

    carry, warmed = lax.fori_loop(0, turns, opening, (carry, zeros), unroll=4)
    for b in range(PIECES):
        if b < PIECES - 2:

            def body(i, state, b=b):
                carry, warmed, ups = state
                return down_rows(b + 1, i, carry), warm_rows(b + 1, i, warmed), up_rows(b, i, ups)

            carry, warmed, _ = lax.fori_loop(0, turns, body, (carry, zeros, warmed), unroll=4)
        elif b == PIECES - 2:

            def body(i, state, b=b):
                carry, ups = state
                return down_rows(b + 1, i, carry), up_rows(b, i, ups)

            carry, _ = lax.fori_loop(0, turns - 1, body, (carry, warmed))
            _ = up_rows(b, turns - 1, _)
            low = seg - GROUP + 2
            for k in range(GROUP):
                row = low + k
                here = [term(c, row) if row < seg else s_buf[c, row] for c in range(3)]
                found, carry = down_row(here, carry)
                for c in range(3):
                    if row < seg:
                        s_buf[c, row] = here[c]
                    o_buf[c, row - 2] = found[c]
        else:
            lax.fori_loop(0, turns, lambda i, ups: up_rows(PIECES - 1, i, ups), last)
        for copy in store(b):
            copy.start()

    def to_rim(k, _):
        for c in range(3):
            rim_ref[c, k] = jnp.where(first, o_buf[c, k], o_buf[c, seg - 1 - k])
        return 0

    lax.fori_loop(0, RIM, to_rim, 0, unroll=8)
    for b in range(PIECES):
        for copy in store(b):
            copy.wait()


def filter_part(terms, local, ups, downs, seg):
    points = 3 * 2 * seg * 4 * LANES
    return pl.pallas_call(
        functools.partial(filter_kernel, seg),
        out_shape=(
            jax.ShapeDtypeStruct((3, 2, seg, 4, LANES), jnp.float32),
            jax.ShapeDtypeStruct((3, RIM, SUBLANES, LANES), jnp.float32),
        ),
        in_specs=[VMEM] * 4,
        out_specs=(HBM, VMEM),
        scratch_shapes=[
            pltpu.VMEM((3, seg + 2, SUBLANES, LANES), jnp.float32),
            pltpu.VMEM((3, seg, SUBLANES, LANES), jnp.float32),
            pltpu.SemaphoreType.DMA((PIECES, 6)),
        ],
        compiler_params=pltpu.CompilerParams(vmem_limit_bytes=24 * 2**20),
        cost_estimate=pl.CostEstimate(flops=20 * points, bytes_accessed=12 * points, transcendentals=0),
        name="compact_filter",
    )(terms, local, ups, downs)


def rim_kernel(seg, o_in, rim_ref, vel_ref, xsums_ref, one_ref, two_ref, o_ref, edge, top, bottom, sems):
    del o_in
    reach = REACH_D
    first = low_rows()
    sign = jnp.where(first, -1.0, 1.0).astype(jnp.float32)
    even = lax.axis_index("gx") % 2 == 0
    edge[:, 0:4, :] = jnp.where(even, two_ref[...], one_ref[...])
    edge[:, 4:8, :] = jnp.where(even, one_ref[...], two_ref[...])
    own = [jnp.where(first, xsums_ref[1, field], xsums_ref[0, field]) for field in range(6)]
    raw = [jnp.where(first, vel_ref[c, 0], vel_ref[c, seg - 1]) for c in range(3)]
    speeds = [SCALE * jnp.where(first, vel_ref[0, k], vel_ref[0, seg - 1 - k]) for k in range(reach)]
    next_to, second = SCALE * edge[6], edge[19]
    for c in range(3):
        bend = (BETA * raw[c]) * (speeds[0] + next_to)
        close = edge[12 + c] - sign * ((own[3 + c] + next_to * own[c]) + bend)
        further = edge[15 + c] - sign * (ROOT_D * (own[3 + c] + second * own[c]))
        gain = 1.0 / (1.0 - ROOT_F * ROOT_D)
        total = edge[9 + c] - sign * ((gain * own[3 + c] + edge[18] * own[c]) + bend)
        change = [
            (sign * ROOT_D**k) * (edge[3 + c] + speeds[k] * edge[c]) for k in range(reach)
        ]
        change[0] = change[0] + sign * ((BETA * edge[6 + c]) * (next_to + speeds[0]))
        line = [further, close] + change + [jnp.zeros_like(close)] * 4
        ups = [None] * reach
        up = jnp.zeros_like(close)
        for k in reversed(range(reach)):
            up = change[k] + ROOT_F * up
            ups[k] = up
        for k in range(RIM):
            scaled = ROOT_F * total
            found = scaled
            if k < reach + 2:
                here = line[k + 2]
                taps = TAP0 * here + TAP1 * (line[k + 1] + line[k + 3]) + TAP2 * (line[k] + line[k + 4])
                found = found + taps
            if k < reach:
                found = found + ups[k]
                total = change[k] + scaled
            else:
                total = scaled
            fixed = rim_ref[c, k] + found
            top[c, k] = fixed
            bottom[c, RIM - 1 - k] = fixed
        pltpu.make_async_copy(top.at[c, :, pl.ds(0, 4)], o_ref.at[c, 0, pl.ds(0, RIM)], sems.at[c, 0]).start()
        pltpu.make_async_copy(
            bottom.at[c, :, pl.ds(4, 4)], o_ref.at[c, 1, pl.ds(seg - RIM, RIM)], sems.at[c, 1]
        ).start()
    for c in range(3):
        pltpu.make_async_copy(top.at[c, :, pl.ds(0, 4)], o_ref.at[c, 0, pl.ds(0, RIM)], sems.at[c, 0]).wait()
        pltpu.make_async_copy(
            bottom.at[c, :, pl.ds(4, 4)], o_ref.at[c, 1, pl.ds(seg - RIM, RIM)], sems.at[c, 1]
        ).wait()


def rim_part(out, rim, vel, xsums, one, two, seg):
    return pl.pallas_call(
        functools.partial(rim_kernel, seg),
        out_shape=jax.ShapeDtypeStruct(out.shape, jnp.float32),
        in_specs=[HBM] + [VMEM] * 5,
        out_specs=HBM,
        input_output_aliases={0: 0},
        scratch_shapes=[
            pltpu.VMEM((20, SUBLANES, LANES), jnp.float32),
            pltpu.VMEM((3, RIM, SUBLANES, LANES), jnp.float32),
            pltpu.VMEM((3, RIM, SUBLANES, LANES), jnp.float32),
            pltpu.SemaphoreType.DMA((3, 2)),
        ],
        compiler_params=pltpu.CompilerParams(vmem_limit_bytes=16 * 2**20),
        name="rim",
    )(out, rim, vel, xsums, one, two)


def ring(axis):
    count = lax.axis_size(axis)
    forward = [(i, (i + 1) % count) for i in range(count)]
    return forward, [(target, source) for source, target in forward]


def pairs(axis):
    count = lax.axis_size(axis)
    one = [(i, i + 1 if i % 2 == 0 else i - 1) for i in range(count)]
    two = [(i, (i - 1 if i % 2 == 0 else i + 1) % count) for i in range(count)]
    return one, two


def blocked(velocity):
    seg = velocity.shape[1] // 2
    vel, numbers = ends(velocity.reshape(3, 2, seg, 4, LANES), seg)
    forward, backward = ring("gz")
    before_z = lax.ppermute(numbers, "gz", forward)
    after_z = lax.ppermute(numbers, "gz", backward)
    local, xsums = x_part(vel, seg)
    terms, ups, downs, one, two = z_part(vel, local, xsums, seg, before_z, after_z)
    first_swap, second_swap = pairs("gx")
    one = lax.ppermute(one, "gx", first_swap)
    two = lax.ppermute(two, "gx", second_swap)
    out, rim = filter_part(terms, local, ups, downs, seg)
    return rim_part(out, rim, vel, xsums, one, two, seg).reshape(velocity.shape)


def with_halo(block, sides, width):
    for axis, dim in sides:
        count = lax.axis_size(axis)
        forward = [(i, i + 1) for i in range(count - 1)]
        forward.append((count - 1, 0))
        backward = [(target, source) for source, target in forward]
        low = lax.ppermute(
            lax.slice_in_dim(block, block.shape[dim] - width, None, axis=dim), axis, forward
        )
        high = lax.ppermute(lax.slice_in_dim(block, 0, width, axis=dim), axis, backward)
        block = jnp.concatenate([low, block, high], axis=dim)
    return block


def tables(length, alpha):
    lower_diag = jnp.concatenate(
        [jnp.zeros((1,), jnp.float32), jnp.full((length - 1,), alpha, jnp.float32)]
    )
    upper_diag = jnp.concatenate(
        [jnp.full((length - 1,), alpha, jnp.float32), jnp.zeros((1,), jnp.float32)]
    )
    main_diag = jnp.ones((length,), jnp.float32)
    identity = jnp.eye(length, dtype=jnp.float32)
    inverse = lax.linalg.tridiagonal_solve(lower_diag, main_diag, upper_diag, identity)
    left_col = alpha * inverse[:, 0]
    right_col = alpha * inverse[:, length - 1]
    coupling = alpha * inverse[0, 0]
    return (inverse, left_col, right_col, coupling)


def offset_slice(extended, offset, length, direction, base=3):
    return lax.slice_in_dim(extended, base + offset, base + offset + length, axis=direction)


def slope_rhs(extended, length, direction, base=3):
    rhs = (
        COEF_A
        * 0.5
        * (
            offset_slice(extended, 1, length, direction, base)
            - offset_slice(extended, -1, length, direction, base)
        )
    )
    return rhs + COEF_B * 0.25 * (
        offset_slice(extended, 2, length, direction, base)
        - offset_slice(extended, -2, length, direction, base)
    )


def smooth_rhs(extended, length, direction, base=3):
    coefficients = filter_coefficients()
    rhs = coefficients[0] * offset_slice(extended, 0, length, direction, base)
    for offset in range(1, 4):
        rhs = rhs + 0.5 * coefficients[offset] * (
            offset_slice(extended, offset, length, direction, base)
            + offset_slice(extended, -offset, length, direction, base)
        )
    return rhs


def wrap_pad(values, direction):
    length = values.shape[direction]
    return jnp.concatenate(
        [
            lax.slice_in_dim(values, length - 3, length, axis=direction),
            values,
            lax.slice_in_dim(values, 0, 3, axis=direction),
        ],
        axis=direction,
    )


def apply_along(inverse, values, direction):
    rotated = jnp.tensordot(
        inverse, values, axes=([1], [direction]), precision=lax.Precision.HIGHEST
    )
    return jnp.moveaxis(rotated, 0, direction)


def end_values(partial_value, direction):
    length = partial_value.shape[direction]
    first_val = lax.slice_in_dim(partial_value, 0, 1, axis=direction)
    last_val = lax.slice_in_dim(partial_value, length - 1, length, axis=direction)
    return (first_val, last_val)


def corrected(partial_value, prev_last, next_first, table, direction):
    inverse, left_col, right_col, coupling = table
    first_val, last_val = end_values(partial_value, direction)
    factor_inv = 1.0 / (1.0 - coupling * coupling)
    left_value = (prev_last - coupling * first_val) * factor_inv
    right_value = (next_first - coupling * last_val) * factor_inv
    dims_list = [1] * partial_value.ndim
    dims_list[direction] = partial_value.shape[direction]
    return (
        partial_value
        - left_col.reshape(dims_list) * left_value
        - right_col.reshape(dims_list) * right_value
    )


def extend_x(values):
    return with_halo(values, (("gx", 1),), 3)


def solve_x(rhs, table):
    partial_value = apply_along(table[0], rhs, 1)
    first_val, last_val = end_values(partial_value, 1)
    beside = with_halo(jnp.concatenate([first_val, last_val], axis=1), (("gx", 1),), 1)
    return corrected(partial_value, beside[:, 0:1], beside[:, 3:4], table, 1)


def solve_blocks(rhs, table):
    dims_list = rhs.shape
    blocks = rhs.reshape(dims_list[:-1] + (dims_list[-1] // block_len, block_len))
    last_dim = blocks.ndim - 1
    partial_value = apply_along(table[0], blocks, last_dim)
    first_val, last_val = end_values(partial_value, last_dim)
    prev_last = jnp.roll(last_val, 1, axis=last_dim - 1)
    next_first = jnp.roll(first_val, -1, axis=last_dim - 1)
    return corrected(partial_value, prev_last, next_first, table, last_dim).reshape(dims_list)


def whole_z_part(velocity):
    slope_z = tables(block_len, ALPHA_D)
    pencil = lax.all_to_all(velocity, "gz", split_axis=1, concat_axis=3, tiled=True)
    along_z = pencil[2:3]
    fields = jnp.concatenate([pencil, along_z * pencil], axis=0)
    slopes = solve_blocks(slope_rhs(wrap_pad(fields, 3), fields.shape[3], 3), slope_z)
    local_terms = slopes[3:] + along_z * slopes[:3]
    return lax.all_to_all(local_terms, "gz", split_axis=3, concat_axis=1, tiled=True)


def per_device(velocity):
    width_x = velocity.shape[1]
    slope_x = tables(width_x, ALPHA_D)
    smooth_x = tables(width_x, ALPHA_F)
    along_x = velocity[0:1]
    rim_source = jnp.concatenate([velocity, along_x * velocity], axis=0)
    padded = extend_x(rim_source)
    slopes_x = solve_x(slope_rhs(padded, width_x, 1), slope_x)
    x_terms = slopes_x[3:] + along_x * slopes_x[:3]
    z_terms = whole_z_part(velocity)
    combined = 0.5 * (x_terms + z_terms)
    smoothed = solve_x(smooth_rhs(extend_x(combined), width_x, 1), smooth_x)
    return -smoothed


def per_block(velocity):
    _, rows, planes, columns = velocity.shape
    fits = planes == 1 and columns == 4 * LANES and rows % 1024 == 0 and lax.axis_size("gx") % 2 == 0
    return blocked(velocity) if fits else per_device(velocity)


def solution(mesh):
    return jax.shard_map(
        per_block,
        mesh=mesh,
        in_specs=(P(None, "gx", None, "gz"),),
        out_specs=P(None, "gx", None, "gz"),
        check_vma=False,
    )
```

```python
import functools

import numpy as np
import jax
import jax.numpy as jnp
from jax import lax
from jax.experimental import pallas as pl
from jax.experimental.pallas import tpu as pltpu
from jax.sharding import PartitionSpec as P

ALPHA_D = 1.0 / 3.0
COEF_A = 14.0 / 9.0
COEF_B = 1.0 / 9.0
ALPHA_F = 0.49
block_len = 128

LANES = 128
SUBLANES = 8
REACH_D = 24
REACH_F = 96
RIM = 128
STEP_ROWS = 128
PIECES = 4
AHEAD = 4
GROUP = 4

ROOT_D = (-1.0 + np.sqrt(1.0 - 4.0 * ALPHA_D**2)) / (2.0 * ALPHA_D)
NEAR_D = COEF_B / (4.0 * ALPHA_D)
GAIN_D = (COEF_A / 2.0 - NEAR_D) * (1.0 - ROOT_D**2) / np.sqrt(1.0 - 4.0 * ALPHA_D**2)
BETA = NEAR_D / GAIN_D


def filter_coefficients():
    return (
        (11.0 + 10.0 * ALPHA_F) / 16.0,
        (15.0 + 34.0 * ALPHA_F) / 32.0,
        (-3.0 + 6.0 * ALPHA_F) / 16.0,
        (1.0 - 2.0 * ALPHA_F) / 32.0,
    )


def split_filter():
    a0, a1, a2, a3 = filter_coefficients()
    poly = [a0 - a2, 0.5 * a1 - 1.5 * a3, 0.5 * a2, 0.5 * a3]
    tap2 = poly[3] / ALPHA_F
    tap1 = (poly[2] - tap2) / ALPHA_F
    tap0 = (poly[1] - tap1) / ALPHA_F
    rest = poly[0] - tap0
    root = (-1.0 + np.sqrt(1.0 - 4.0 * ALPHA_F**2)) / (2.0 * ALPHA_F)
    gain = rest / np.sqrt(1.0 - 4.0 * ALPHA_F**2)
    return root, gain, (tap0 + 2.0 * tap2) / gain, tap1 / gain, tap2 / gain


ROOT_F, GAIN_F, TAP0, TAP1, TAP2 = (float(v) for v in split_filter())
ROOT_D, GAIN_D, BETA = float(ROOT_D), float(GAIN_D), float(BETA)
SCALE = -0.5 * GAIN_D * GAIN_F


def line_table():
    lane = np.arange(LANES)

    def kernel(offset):
        size = np.abs(offset)
        return np.sign(offset) * (ROOT_D ** (np.maximum(size, 1) - 1.0) + BETA * (size == 1))

    inside = kernel(lane[:, None] - lane[None, :])
    source = np.where(lane < LANES // 2, lane + LANES, lane - LANES)
    beside = kernel(source[:, None] - lane[None, :])
    return (SCALE * np.concatenate([inside, beside], axis=0)).astype(np.float32)


def end_table():
    row = lax.broadcasted_iota(jnp.int32, (LANES, LANES), 0)
    lane = lax.broadcasted_iota(jnp.int32, (LANES, LANES), 1)
    starts = row < LANES // 2
    steps = jnp.where(starts, row - 1, LANES - 2 - row)
    size = jnp.exp(float(np.log(-ROOT_D)) * jnp.maximum(steps, 0).astype(jnp.float32))
    power = jnp.where(steps % 2 == 0, size, -size)
    inner = (steps >= 0) & (lane == jnp.where(starts, 3, 0))
    edge = (steps < 0) & (lane == jnp.where(starts, 2, 1))
    return jnp.where(inner, power, jnp.where(edge, 1.0, 0.0))


def split_value(value):
    high = value.astype(jnp.bfloat16)
    low = (value - high.astype(jnp.float32)).astype(jnp.bfloat16)
    return high, low


def low_rows():
    return lax.broadcasted_iota(jnp.int32, (SUBLANES, LANES), 0) < SUBLANES // 2


def low_lanes(rows):
    return lax.broadcasted_iota(jnp.int32, (rows, LANES), 1) < LANES // 2


def six_fields(factor, parts):
    return list(parts) + [factor * part for part in parts]


def ends_kernel(seg, v_ref, vel_ref, numbers_ref, weights, sems):
    rows = LANES
    count = seg // rows

    def load(b):
        at = pl.ds(b * rows, rows)
        return [
            pltpu.make_async_copy(v_ref.at[c, h, at], vel_ref.at[c, at, pl.ds(4 * h, 4)], sems.at[b, 2 * c + h])
            for c in range(3)
            for h in range(2)
        ]

    for b in range(AHEAD):
        for copy in load(b):
            copy.start()
    table = end_table()
    for field in range(6):
        moved = table if field == 0 else pltpu.roll(table, 4 * field, axis=1)
        high, low = split_value(moved)
        for part in range(2):
            at = pl.ds((2 * field + part) * LANES, LANES)
            weights[at, 0:LANES] = high
            weights[at, LANES:] = low
    low_lane = low_lanes(2 * rows)
    flat = vel_ref.reshape(3 * seg * SUBLANES, LANES)

    for b in range(count):
        for copy in load(b):
            copy.wait()
        if b + AHEAD < count:
            for copy in load(b + AHEAD):
                copy.start()
        parts = []
        for c in range(3):
            start, end = (
                jnp.concatenate(
                    [
                        flat[pl.ds((c * seg + b * rows + 8 * k) * SUBLANES + 4 * h + n, 8, stride=SUBLANES), :]
                        for h in range(2)
                        for k in range(rows // 8)
                    ],
                    axis=0,
                )
                for n in (0, 3)
            )
            parts.append(jnp.where(low_lane, start, end))
        pieces = []
        for field in six_fields(parts[2], parts):
            pieces += list(split_value(field))
        both = jnp.dot(jnp.concatenate(pieces, axis=1), weights[...], preferred_element_type=jnp.float32)
        numbers = both[:, :LANES] + both[:, LANES:]
        for h in range(2):
            turned = numbers[h * rows : (h + 1) * rows].T
            numbers_ref[:, pl.ds(h * seg + b * rows, rows)] = turned[0:24]


HBM = pl.BlockSpec(memory_space=pl.ANY)
VMEM = pl.BlockSpec(memory_space=pltpu.VMEM)


def ends(view, seg):
    return pl.pallas_call(
        functools.partial(ends_kernel, seg),
        out_shape=(
            jax.ShapeDtypeStruct((3, seg, SUBLANES, LANES), jnp.float32),
            jax.ShapeDtypeStruct((24, 2 * seg), jnp.float32),
        ),
        in_specs=[HBM],
        out_specs=(VMEM, VMEM),
        scratch_shapes=[
            pltpu.VMEM((12 * LANES, 2 * LANES), jnp.bfloat16),
            pltpu.SemaphoreType.DMA((seg // LANES, 6)),
        ],
        compiler_params=pltpu.CompilerParams(vmem_limit_bytes=44 * 2**20),
        name="line_ends",
    )(view)


def x_kernel(seg, vel_ref, s_ref, sums_ref):
    reach = REACH_D
    first = low_rows()
    zero = jnp.zeros((SUBLANES, LANES), jnp.float32)
    start = ((zero,) * 6, (zero,) * 4)

    def advance(values, carry):
        sums, near = carry
        speed = SCALE * values[0]
        terms = six_fields(speed, values)
        bend = BETA * (near[3] + speed)
        found = [(sums[3 + c] + speed * sums[c]) + near[c] * bend for c in range(3)]
        return found, (tuple(term + ROOT_D * total for term, total in zip(terms, sums)), (*values, speed))

    def row(i):
        return [vel_ref[c, i] for c in range(3)]

    def other(i, keep_first):
        turned = [pltpu.roll(value, 4, axis=0) for value in row(i)]
        return [jnp.where(first, value, 0.0) if keep_first else jnp.where(first, 0.0, value) for value in turned]

    def forward(i, carry):
        found, carry = advance(row(i), carry)
        for c in range(3):
            s_ref[c, i] = found[c]
        return carry

    def backward(k, carry):
        i = seg - 1 - k
        found, carry = advance(row(i), carry)
        for c in range(3):
            s_ref[c, i] = found[c] - s_ref[c, i]
        return carry

    carry = lax.fori_loop(0, reach, lambda i, k: advance(other(seg - reach + i, False), k)[1], start, unroll=8)
    carry = lax.fori_loop(0, seg, forward, carry, unroll=16)
    for field in range(6):
        sums_ref[0, field] = carry[0][field]
    carry = lax.fori_loop(0, reach, lambda i, k: advance(other(reach - 1 - i, True), k)[1], start, unroll=8)
    carry = lax.fori_loop(0, seg, backward, carry, unroll=16)
    for field in range(6):
        sums_ref[1, field] = carry[0][field]


def x_part(vel, seg):
    points = 3 * 2 * seg * 4 * LANES
    return pl.pallas_call(
        functools.partial(x_kernel, seg),
        out_shape=(
            jax.ShapeDtypeStruct(vel.shape, jnp.float32),
            jax.ShapeDtypeStruct((2, 6, SUBLANES, LANES), jnp.float32),
        ),
        in_specs=[VMEM],
        out_specs=(VMEM, VMEM),
        compiler_params=pltpu.CompilerParams(vmem_limit_bytes=16 * 2**20),
        cost_estimate=pl.CostEstimate(flops=60 * points, bytes_accessed=8 * points, transcendentals=0),
        name="x_slopes",
    )(vel)


def z_kernel(
    seg, vel_ref, sx_ref, xsums_ref, table_ref, zl_ref, zr_ref,
    sbuf, ups_ref, downs_ref, one_ref, two_ref,
    weights, turn, halo_hi, halo_lo, pack,
):
    far = REACH_F
    step_rows = STEP_ROWS
    rows = 2 * step_rows
    first = low_rows()
    flat = vel_ref.reshape(3 * seg * SUBLANES, LANES)

    for part in range(2):
        high, low = split_value(table_ref[part * LANES : (part + 1) * LANES, :])
        for copy in range(2):
            at = pl.ds((2 * part + copy) * LANES, LANES)
            weights[at, 0:LANES] = high
            weights[at, LANES:] = low

    lane = lax.broadcasted_iota(jnp.int32, (LANES, LANES), 1)
    outer_lane = (lane >= LANES - 2) | (lane < 2)
    from_before = lax.broadcasted_iota(jnp.int32, (24, LANES), 0) % 4 < 2
    turn[24:, :] = jnp.zeros((LANES - 24, LANES), jnp.float32)
    for part in range(2 * seg // LANES):
        at = pl.ds(part * LANES, LANES)
        turn[0:24, :] = jnp.where(from_before, zl_ref[:, at], zr_ref[:, at])
        numbers = turn[...].T
        for field in range(6):
            moved = pltpu.roll(numbers, LANES - 2 - 4 * field, axis=1)
            high, low = split_value(jnp.where(outer_lane, moved, 0.0))
            halo_hi[field, at, :] = high
            halo_lo[field, at, :] = low

    along_x = sx_ref.reshape(3 * seg * SUBLANES, LANES)
    low_lane = jnp.where(low_lanes(rows), 1.0, 0.0).astype(jnp.bfloat16) > 0.5

    def strided(c, xi, n):
        return jnp.concatenate(
            [
                flat[pl.ds((c * seg + xi + 8 * k) * SUBLANES + 4 * h + n, 8, stride=SUBLANES), :]
                for h in range(2)
                for k in range(step_rows // 8)
            ],
            axis=0,
        )

    def build(step):
        store = {}
        xi = pl.multiple_of(step * step_rows, step_rows)
        along = [[strided(c, xi, n) for c in range(3)] for n in range(4)]
        for field in range(6):
            halves = []
            for n in range(4):
                value = along[n][field % 3]
                halves.append(split_value(along[n][2] * value if field >= 3 else value))
            for which, halo in ((0, halo_hi), (1, halo_lo)):
                outer = jnp.concatenate(
                    [halo[field, pl.ds(pl.multiple_of(h * seg + xi, 16), step_rows), :] for h in range(2)], axis=0
                )
                line = [outer] + [pair[which] for pair in halves] + [outer]
                for n in range(4):
                    at = pl.ds(((field % 3 * 4 + n) * 2 + field // 3) * rows, rows)
                    store[(field % 3 * 4 + n) * 2 + field // 3, which] = line[n + 1]
                    store[(field % 3 * 4 + n) * 2 + field // 3, 2 + which] = jnp.where(low_lane, line[n + 2], line[n])
        return jnp.concatenate([jnp.concatenate([store[q, p] for p in range(4)], axis=1) for q in range(24)], axis=0)

    def finish(step, both):
        xi = pl.multiple_of(step * step_rows, step_rows)
        alongs = [strided(2, xi, n) for n in range(4)]
        for c in range(3):
            for n in range(4):
                along = alongs[n]
                base = (c * 4 + n) * 2 * rows
                plain = both[base : base + rows]
                mixed = both[base + rows : base + 2 * rows]
                term = (mixed[:, :LANES] + mixed[:, LANES:]) + along * (plain[:, :LANES] + plain[:, LANES:])
                for h in range(2):
                    for k in range(step_rows // 8):
                        at = (c * seg + xi + 8 * k) * SUBLANES + 4 * h + n
                        piece = h * (step_rows // 8) + k
                        at = pl.ds(at, 8, stride=SUBLANES)
                        sbuf[at, :] = term[piece * 8 : piece * 8 + 8] + along_x[at, :]

    zero = jnp.zeros((SUBLANES, LANES), jnp.float32)

    def block(step, _):
        finish(step, jnp.dot(build(step), weights[...], preferred_element_type=jnp.float32))
        return 0

    lax.fori_loop(0, seg // step_rows, block, 0)

    def row_of(c, row):
        at = pl.ds(pl.multiple_of((c * seg + row) * SUBLANES, SUBLANES), SUBLANES)
        return sbuf[at, :]

    def sums_of(k, sums):
        ups, downs = sums
        ups = tuple(row_of(c, far - 1 - k) + ROOT_F * ups[c] for c in range(3))
        downs = tuple(row_of(c, seg - far + k) + ROOT_F * downs[c] for c in range(3))
        return ups, downs

    ups, downs = lax.fori_loop(0, far, sums_of, ((zero,) * 3,) * 2, unroll=8)
    for c in range(3):
        ups_ref[c] = ups[c]
        downs_ref[c] = downs[c]

    for field in range(6):
        pack[field] = jnp.where(first, xsums_ref[1, field], xsums_ref[0, field])
    for c in range(3):
        pack[6 + c] = jnp.where(first, vel_ref[c, 0], vel_ref[c, seg - 1])
        pack[9 + c] = jnp.where(first, ups[c], downs[c])
        pack[12 + c] = jnp.where(first, row_of(c, 0), row_of(c, seg - 1))
        pack[15 + c] = jnp.where(first, row_of(c, 1), row_of(c, seg - 2))
    weighted = zero
    for k in reversed(range(REACH_D)):
        weighted = jnp.where(first, vel_ref[0, k], vel_ref[0, seg - 1 - k]) + (ROOT_F * ROOT_D) * weighted
    pack[18] = SCALE * weighted
    pack[19] = SCALE * jnp.where(first, vel_ref[0, 1], vel_ref[0, seg - 2])
    even = lax.axis_index("gx") % 2 == 0
    one_ref[...] = jnp.where(even, pack[:, 4:8, :], pack[:, 0:4, :])
    two_ref[...] = jnp.where(even, pack[:, 0:4, :], pack[:, 4:8, :])


def z_part(vel, local, xsums, seg, before_z, after_z):
    side = jax.ShapeDtypeStruct((20, 4, LANES), jnp.float32)
    return pl.pallas_call(
        functools.partial(z_kernel, seg),
        out_shape=(
            jax.ShapeDtypeStruct((3 * seg * SUBLANES, LANES), jnp.float32),
            jax.ShapeDtypeStruct((3, SUBLANES, LANES), jnp.float32),
            jax.ShapeDtypeStruct((3, SUBLANES, LANES), jnp.float32),
            side,
            side,
        ),
        in_specs=[VMEM] * 6,
        out_specs=(VMEM,) * 5,
        scratch_shapes=[
            pltpu.VMEM((4 * LANES, 2 * LANES), jnp.bfloat16),
            pltpu.VMEM((LANES, LANES), jnp.float32),
            pltpu.VMEM((6, 2 * seg, LANES), jnp.bfloat16),
            pltpu.VMEM((6, 2 * seg, LANES), jnp.bfloat16),
            pltpu.VMEM((20, SUBLANES, LANES), jnp.float32),
        ],
        compiler_params=pltpu.CompilerParams(vmem_limit_bytes=28 * 2**20),
        name="z_slopes",
    )(vel, local, xsums, jnp.asarray(line_table()), before_z, after_z)


def filter_kernel(seg, s_ref, ups_ref, downs_ref, o_ref, rim_ref, o_buf, sems):
    size = seg // PIECES
    turns = size // GROUP
    warm_group = REACH_F // turns
    first = low_rows()

    def term(c, row):
        at = pl.ds(pl.multiple_of((c * seg + row) * SUBLANES, SUBLANES), SUBLANES)
        return s_ref[at, :]

    def to_second(value):
        return jnp.where(first, 0.0, pltpu.roll(value, 4, axis=0))

    def to_first(value):
        return jnp.where(first, pltpu.roll(value, 4, axis=0), 0.0)

    def down_row(here, carry):
        found, out = [], []
        for c in range(3):
            down, scaled1, scaled2, one, two, three, four = carry[c]
            scaled = ROOT_F * down
            taps = TAP0 * two + TAP1 * (one + three) + TAP2 * (here[c] + four)
            found.append(scaled2 + taps)
            out.append((here[c] + scaled, scaled, scaled1, here[c], one, two, three))
        return found, tuple(out)

    def down_rows(b, i, carry):
        low = b * size + 2 + GROUP * i
        count = GROUP
        lines = [[term(c, low + k) for c in range(3)] for k in range(count)]
        results = []
        for here in lines:
            found, carry = down_row(here, carry)
            results.append(found)
        for k in range(count):
            for c in range(3):
                o_buf[c, low + k - 2] = results[k][c]
        return carry

    def warm_rows(b, i, ups):
        top = (b + 1) * size + REACH_F - 1 - warm_group * i
        lines = [[term(c, top - k) for c in range(3)] for k in range(warm_group)]
        for here in lines:
            ups = tuple(here[c] + ROOT_F * ups[c] for c in range(3))
        return ups

    def up_rows(b, i, ups):
        low = (b + 1) * size - GROUP * (i + 1)
        order = list(reversed(range(GROUP)))
        here = {(k, c): term(c, low + k) for k in order for c in range(3)}
        found = {(k, c): o_buf[c, low + k] for k in order for c in range(3)}
        for k in order:
            ups = tuple(here[k, c] + ROOT_F * ups[c] for c in range(3))
            for c in range(3):
                found[k, c] = found[k, c] + ups[c]
        for k in order:
            for c in range(3):
                o_buf[c, low + k] = found[k, c]
        return ups

    def store(b):
        at = pl.ds(b * size, size)
        edge = RIM // size
        return [
            pltpu.make_async_copy(o_buf.at[c, at, pl.ds(4 * h, 4)], o_ref.at[c, h, at], sems.at[b, 2 * c + h])
            for c in range(3)
            for h in range(2)
            if (b >= edge if h == 0 else b < PIECES - edge)
        ]

    zero = jnp.zeros((SUBLANES, LANES), jnp.float32)
    zeros = (zero,) * 3
    carry = tuple(
        (
            to_second(downs_ref[c]), zero, zero,
            to_second(term(c, seg - 1)), to_second(term(c, seg - 2)), zero, zero,
        )
        for c in range(3)
    )
    for k in range(2):
        carry = down_row([term(c, k) for c in range(3)], carry)[1]
    last = tuple(to_first(ups_ref[c]) for c in range(3))

    def opening(i, state):
        carry, warmed = state
        return down_rows(0, i, carry), warm_rows(0, i, warmed)

    carry, warmed = lax.fori_loop(0, turns, opening, (carry, zeros), unroll=4)
    for b in range(PIECES):
        if b < PIECES - 2:

            def body(i, state, b=b):
                carry, warmed, ups = state
                return down_rows(b + 1, i, carry), warm_rows(b + 1, i, warmed), up_rows(b, i, ups)

            carry, warmed, _ = lax.fori_loop(0, turns, body, (carry, zeros, warmed), unroll=4)
        elif b == PIECES - 2:

            def body(i, state, b=b):
                carry, ups = state
                return down_rows(b + 1, i, carry), up_rows(b, i, ups)

            carry, _ = lax.fori_loop(0, turns - 1, body, (carry, warmed), unroll=4)
            _ = up_rows(b, turns - 1, _)
            low = seg - GROUP + 2
            for k in range(GROUP):
                row = low + k
                here = [term(c, row) if row < seg else to_first(term(c, row - seg)) for c in range(3)]
                found, carry = down_row(here, carry)
                for c in range(3):
                    o_buf[c, row - 2] = found[c]
        else:
            lax.fori_loop(0, turns, lambda i, ups: up_rows(PIECES - 1, i, ups), last, unroll=4)
        for copy in store(b):
            copy.start()

    def to_rim(k, _):
        for c in range(3):
            rim_ref[c, k] = jnp.where(first, o_buf[c, k], o_buf[c, seg - 1 - k])
        return 0

    lax.fori_loop(0, RIM, to_rim, 0, unroll=8)
    for b in range(PIECES):
        for copy in store(b):
            copy.wait()


def filter_part(terms, ups, downs, seg):
    points = 3 * 2 * seg * 4 * LANES
    return pl.pallas_call(
        functools.partial(filter_kernel, seg),
        out_shape=(
            jax.ShapeDtypeStruct((3, 2, seg, 4, LANES), jnp.float32),
            jax.ShapeDtypeStruct((3, RIM, SUBLANES, LANES), jnp.float32),
        ),
        in_specs=[VMEM] * 3,
        out_specs=(HBM, VMEM),
        scratch_shapes=[
            pltpu.VMEM((3, seg, SUBLANES, LANES), jnp.float32),
            pltpu.SemaphoreType.DMA((PIECES, 6)),
        ],
        compiler_params=pltpu.CompilerParams(vmem_limit_bytes=24 * 2**20),
        cost_estimate=pl.CostEstimate(flops=20 * points, bytes_accessed=12 * points, transcendentals=0),
        name="compact_filter",
    )(terms, ups, downs)


def rim_kernel(seg, o_in, rim_ref, vel_ref, xsums_ref, one_ref, two_ref, o_ref, edge, top, bottom, sems):
    del o_in
    reach = REACH_D
    first = low_rows()
    sign = jnp.where(first, -1.0, 1.0).astype(jnp.float32)
    even = lax.axis_index("gx") % 2 == 0
    edge[:, 0:4, :] = jnp.where(even, two_ref[...], one_ref[...])
    edge[:, 4:8, :] = jnp.where(even, one_ref[...], two_ref[...])
    own = [jnp.where(first, xsums_ref[1, field], xsums_ref[0, field]) for field in range(6)]
    raw = [jnp.where(first, vel_ref[c, 0], vel_ref[c, seg - 1]) for c in range(3)]
    speeds = [SCALE * jnp.where(first, vel_ref[0, k], vel_ref[0, seg - 1 - k]) for k in range(reach)]
    next_to, second = SCALE * edge[6], edge[19]
    for c in range(3):
        bend = (BETA * raw[c]) * (speeds[0] + next_to)
        close = edge[12 + c] - sign * ((own[3 + c] + next_to * own[c]) + bend)
        further = edge[15 + c] - sign * (ROOT_D * (own[3 + c] + second * own[c]))
        gain = 1.0 / (1.0 - ROOT_F * ROOT_D)
        total = edge[9 + c] - sign * ((gain * own[3 + c] + edge[18] * own[c]) + bend)
        change = [
            (sign * ROOT_D**k) * (edge[3 + c] + speeds[k] * edge[c]) for k in range(reach)
        ]
        change[0] = change[0] + sign * ((BETA * edge[6 + c]) * (next_to + speeds[0]))
        line = [further, close] + change + [jnp.zeros_like(close)] * 4
        ups = [None] * reach
        up = jnp.zeros_like(close)
        for k in reversed(range(reach)):
            up = change[k] + ROOT_F * up
            ups[k] = up
        for k in range(RIM):
            scaled = ROOT_F * total
            found = scaled
            if k < reach + 2:
                here = line[k + 2]
                taps = TAP0 * here + TAP1 * (line[k + 1] + line[k + 3]) + TAP2 * (line[k] + line[k + 4])
                found = found + taps
            if k < reach:
                found = found + ups[k]
                total = change[k] + scaled
            else:
                total = scaled
            fixed = rim_ref[c, k] + found
            top[c, k] = fixed
            bottom[c, RIM - 1 - k] = fixed
        pltpu.make_async_copy(top.at[c, :, pl.ds(0, 4)], o_ref.at[c, 0, pl.ds(0, RIM)], sems.at[c, 0]).start()
        pltpu.make_async_copy(
            bottom.at[c, :, pl.ds(4, 4)], o_ref.at[c, 1, pl.ds(seg - RIM, RIM)], sems.at[c, 1]
        ).start()
    for c in range(3):
        pltpu.make_async_copy(top.at[c, :, pl.ds(0, 4)], o_ref.at[c, 0, pl.ds(0, RIM)], sems.at[c, 0]).wait()
        pltpu.make_async_copy(
            bottom.at[c, :, pl.ds(4, 4)], o_ref.at[c, 1, pl.ds(seg - RIM, RIM)], sems.at[c, 1]
        ).wait()


def rim_part(out, rim, vel, xsums, one, two, seg):
    return pl.pallas_call(
        functools.partial(rim_kernel, seg),
        out_shape=jax.ShapeDtypeStruct(out.shape, jnp.float32),
        in_specs=[HBM] + [VMEM] * 5,
        out_specs=HBM,
        input_output_aliases={0: 0},
        scratch_shapes=[
            pltpu.VMEM((20, SUBLANES, LANES), jnp.float32),
            pltpu.VMEM((3, RIM, SUBLANES, LANES), jnp.float32),
            pltpu.VMEM((3, RIM, SUBLANES, LANES), jnp.float32),
            pltpu.SemaphoreType.DMA((3, 2)),
        ],
        compiler_params=pltpu.CompilerParams(vmem_limit_bytes=16 * 2**20),
        name="rim",
    )(out, rim, vel, xsums, one, two)


def ring(axis):
    count = lax.axis_size(axis)
    forward = [(i, (i + 1) % count) for i in range(count)]
    return forward, [(target, source) for source, target in forward]


def pairs(axis):
    count = lax.axis_size(axis)
    one = [(i, i + 1 if i % 2 == 0 else i - 1) for i in range(count)]
    two = [(i, (i - 1 if i % 2 == 0 else i + 1) % count) for i in range(count)]
    return one, two


def blocked(velocity):
    seg = velocity.shape[1] // 2
    vel, numbers = ends(velocity.reshape(3, 2, seg, 4, LANES), seg)
    forward, backward = ring("gz")
    before_z = lax.ppermute(numbers, "gz", forward)
    after_z = lax.ppermute(numbers, "gz", backward)
    local, xsums = x_part(vel, seg)
    terms, ups, downs, one, two = z_part(vel, local, xsums, seg, before_z, after_z)
    first_swap, second_swap = pairs("gx")
    one = lax.ppermute(one, "gx", first_swap)
    two = lax.ppermute(two, "gx", second_swap)
    out, rim = filter_part(terms, ups, downs, seg)
    return rim_part(out, rim, vel, xsums, one, two, seg).reshape(velocity.shape)


def with_halo(block, sides, width):
    for axis, dim in sides:
        count = lax.axis_size(axis)
        forward = [(i, i + 1) for i in range(count - 1)]
        forward.append((count - 1, 0))
        backward = [(target, source) for source, target in forward]
        low = lax.ppermute(
            lax.slice_in_dim(block, block.shape[dim] - width, None, axis=dim), axis, forward
        )
        high = lax.ppermute(lax.slice_in_dim(block, 0, width, axis=dim), axis, backward)
        block = jnp.concatenate([low, block, high], axis=dim)
    return block


def tables(length, alpha):
    lower_diag = jnp.concatenate(
        [jnp.zeros((1,), jnp.float32), jnp.full((length - 1,), alpha, jnp.float32)]
    )
    upper_diag = jnp.concatenate(
        [jnp.full((length - 1,), alpha, jnp.float32), jnp.zeros((1,), jnp.float32)]
    )
    main_diag = jnp.ones((length,), jnp.float32)
    identity = jnp.eye(length, dtype=jnp.float32)
    inverse = lax.linalg.tridiagonal_solve(lower_diag, main_diag, upper_diag, identity)
    left_col = alpha * inverse[:, 0]
    right_col = alpha * inverse[:, length - 1]
    coupling = alpha * inverse[0, 0]
    return (inverse, left_col, right_col, coupling)


def offset_slice(extended, offset, length, direction, base=3):
    return lax.slice_in_dim(extended, base + offset, base + offset + length, axis=direction)


def slope_rhs(extended, length, direction, base=3):
    rhs = (
        COEF_A
        * 0.5
        * (
            offset_slice(extended, 1, length, direction, base)
            - offset_slice(extended, -1, length, direction, base)
        )
    )
    return rhs + COEF_B * 0.25 * (
        offset_slice(extended, 2, length, direction, base)
        - offset_slice(extended, -2, length, direction, base)
    )


def smooth_rhs(extended, length, direction, base=3):
    coefficients = filter_coefficients()
    rhs = coefficients[0] * offset_slice(extended, 0, length, direction, base)
    for offset in range(1, 4):
        rhs = rhs + 0.5 * coefficients[offset] * (
            offset_slice(extended, offset, length, direction, base)
            + offset_slice(extended, -offset, length, direction, base)
        )
    return rhs


def wrap_pad(values, direction):
    length = values.shape[direction]
    return jnp.concatenate(
        [
            lax.slice_in_dim(values, length - 3, length, axis=direction),
            values,
            lax.slice_in_dim(values, 0, 3, axis=direction),
        ],
        axis=direction,
    )


def apply_along(inverse, values, direction):
    rotated = jnp.tensordot(
        inverse, values, axes=([1], [direction]), precision=lax.Precision.HIGHEST
    )
    return jnp.moveaxis(rotated, 0, direction)


def end_values(partial_value, direction):
    length = partial_value.shape[direction]
    first_val = lax.slice_in_dim(partial_value, 0, 1, axis=direction)
    last_val = lax.slice_in_dim(partial_value, length - 1, length, axis=direction)
    return (first_val, last_val)


def corrected(partial_value, prev_last, next_first, table, direction):
    inverse, left_col, right_col, coupling = table
    first_val, last_val = end_values(partial_value, direction)
    factor_inv = 1.0 / (1.0 - coupling * coupling)
    left_value = (prev_last - coupling * first_val) * factor_inv
    right_value = (next_first - coupling * last_val) * factor_inv
    dims_list = [1] * partial_value.ndim
    dims_list[direction] = partial_value.shape[direction]
    return (
        partial_value
        - left_col.reshape(dims_list) * left_value
        - right_col.reshape(dims_list) * right_value
    )


def extend_x(values):
    return with_halo(values, (("gx", 1),), 3)


def solve_x(rhs, table):
    partial_value = apply_along(table[0], rhs, 1)
    first_val, last_val = end_values(partial_value, 1)
    beside = with_halo(jnp.concatenate([first_val, last_val], axis=1), (("gx", 1),), 1)
    return corrected(partial_value, beside[:, 0:1], beside[:, 3:4], table, 1)


def solve_blocks(rhs, table):
    dims_list = rhs.shape
    blocks = rhs.reshape(dims_list[:-1] + (dims_list[-1] // block_len, block_len))
    last_dim = blocks.ndim - 1
    partial_value = apply_along(table[0], blocks, last_dim)
    first_val, last_val = end_values(partial_value, last_dim)
    prev_last = jnp.roll(last_val, 1, axis=last_dim - 1)
    next_first = jnp.roll(first_val, -1, axis=last_dim - 1)
    return corrected(partial_value, prev_last, next_first, table, last_dim).reshape(dims_list)


def whole_z_part(velocity):
    slope_z = tables(block_len, ALPHA_D)
    pencil = lax.all_to_all(velocity, "gz", split_axis=1, concat_axis=3, tiled=True)
    along_z = pencil[2:3]
    fields = jnp.concatenate([pencil, along_z * pencil], axis=0)
    slopes = solve_blocks(slope_rhs(wrap_pad(fields, 3), fields.shape[3], 3), slope_z)
    local_terms = slopes[3:] + along_z * slopes[:3]
    return lax.all_to_all(local_terms, "gz", split_axis=3, concat_axis=1, tiled=True)


def per_device(velocity):
    width_x = velocity.shape[1]
    slope_x = tables(width_x, ALPHA_D)
    smooth_x = tables(width_x, ALPHA_F)
    along_x = velocity[0:1]
    rim_source = jnp.concatenate([velocity, along_x * velocity], axis=0)
    padded = extend_x(rim_source)
    slopes_x = solve_x(slope_rhs(padded, width_x, 1), slope_x)
    x_terms = slopes_x[3:] + along_x * slopes_x[:3]
    z_terms = whole_z_part(velocity)
    combined = 0.5 * (x_terms + z_terms)
    smoothed = solve_x(smooth_rhs(extend_x(combined), width_x, 1), smooth_x)
    return -smoothed


def per_block(velocity):
    _, rows, planes, columns = velocity.shape
    fits = planes == 1 and columns == 4 * LANES and rows % 1024 == 0 and lax.axis_size("gx") % 2 == 0
    return blocked(velocity) if fits else per_device(velocity)


def solution(mesh):
    return jax.shard_map(
        per_block,
        mesh=mesh,
        in_specs=(P(None, "gx", None, "gz"),),
        out_specs=P(None, "gx", None, "gz"),
        check_vma=False,
    )
```

```python
import functools

import numpy as np
import jax
import jax.numpy as jnp
from jax import lax
from jax.experimental import pallas as pl
from jax.experimental.pallas import tpu as pltpu
from jax.sharding import PartitionSpec as P

ALPHA_D = 1.0 / 3.0
COEF_A = 14.0 / 9.0
COEF_B = 1.0 / 9.0
ALPHA_F = 0.49
block_len = 128

LANES = 128
SUBLANES = 8
REACH_D = 24
REACH_F = 96
RIM = 128
STEP_ROWS = 128
PIECES = 4
AHEAD = 4
GROUP = 4

ROOT_D = (-1.0 + np.sqrt(1.0 - 4.0 * ALPHA_D**2)) / (2.0 * ALPHA_D)
NEAR_D = COEF_B / (4.0 * ALPHA_D)
GAIN_D = (COEF_A / 2.0 - NEAR_D) * (1.0 - ROOT_D**2) / np.sqrt(1.0 - 4.0 * ALPHA_D**2)
BETA = NEAR_D / GAIN_D


def filter_coefficients():
    return (
        (11.0 + 10.0 * ALPHA_F) / 16.0,
        (15.0 + 34.0 * ALPHA_F) / 32.0,
        (-3.0 + 6.0 * ALPHA_F) / 16.0,
        (1.0 - 2.0 * ALPHA_F) / 32.0,
    )


def split_filter():
    a0, a1, a2, a3 = filter_coefficients()
    poly = [a0 - a2, 0.5 * a1 - 1.5 * a3, 0.5 * a2, 0.5 * a3]
    tap2 = poly[3] / ALPHA_F
    tap1 = (poly[2] - tap2) / ALPHA_F
    tap0 = (poly[1] - tap1) / ALPHA_F
    rest = poly[0] - tap0
    root = (-1.0 + np.sqrt(1.0 - 4.0 * ALPHA_F**2)) / (2.0 * ALPHA_F)
    gain = rest / np.sqrt(1.0 - 4.0 * ALPHA_F**2)
    return root, gain, (tap0 + 2.0 * tap2) / gain, tap1 / gain, tap2 / gain


ROOT_F, GAIN_F, TAP0, TAP1, TAP2 = (float(v) for v in split_filter())
ROOT_D, GAIN_D, BETA = float(ROOT_D), float(GAIN_D), float(BETA)
SCALE = -0.5 * GAIN_D * GAIN_F


def line_table():
    lane = np.arange(LANES)

    def kernel(offset):
        size = np.abs(offset)
        return np.sign(offset) * (ROOT_D ** (np.maximum(size, 1) - 1.0) + BETA * (size == 1))

    inside = kernel(lane[:, None] - lane[None, :])
    source = np.where(lane < LANES // 2, lane + LANES, lane - LANES)
    beside = kernel(source[:, None] - lane[None, :])
    return (SCALE * np.concatenate([inside, beside], axis=0)).astype(np.float32)


def end_table():
    row = lax.broadcasted_iota(jnp.int32, (LANES, LANES), 0)
    lane = lax.broadcasted_iota(jnp.int32, (LANES, LANES), 1)
    starts = row < LANES // 2
    steps = jnp.where(starts, row - 1, LANES - 2 - row)
    size = jnp.exp(float(np.log(-ROOT_D)) * jnp.maximum(steps, 0).astype(jnp.float32))
    power = jnp.where(steps % 2 == 0, size, -size)
    inner = (steps >= 0) & (lane == jnp.where(starts, 3, 0))
    edge = (steps < 0) & (lane == jnp.where(starts, 2, 1))
    return jnp.where(inner, power, jnp.where(edge, 1.0, 0.0))


def split_value(value):
    high = value.astype(jnp.bfloat16)
    low = (value - high.astype(jnp.float32)).astype(jnp.bfloat16)
    return high, low


def low_rows():
    return lax.broadcasted_iota(jnp.int32, (SUBLANES, LANES), 0) < SUBLANES // 2


def low_lanes(rows):
    return lax.broadcasted_iota(jnp.int32, (rows, LANES), 1) < LANES // 2


def six_fields(factor, parts):
    return list(parts) + [factor * part for part in parts]


def ends_kernel(seg, v_ref, vel_ref, numbers_ref, weights, sems):
    rows = LANES
    count = seg // rows

    def load(b):
        at = pl.ds(b * rows, rows)
        return [
            pltpu.make_async_copy(v_ref.at[c, h, at], vel_ref.at[c, at, pl.ds(4 * h, 4)], sems.at[b, 2 * c + h])
            for c in range(3)
            for h in range(2)
        ]

    for b in range(AHEAD):
        for copy in load(b):
            copy.start()
    table = end_table()
    for field in range(6):
        moved = table if field == 0 else pltpu.roll(table, 4 * field, axis=1)
        high, low = split_value(moved)
        for part in range(2):
            at = pl.ds((2 * field + part) * LANES, LANES)
            weights[at, 0:LANES] = high
            weights[at, LANES:] = low
    low_lane = low_lanes(2 * rows)
    flat = vel_ref.reshape(3 * seg * SUBLANES, LANES)

    for b in range(count):
        for copy in load(b):
            copy.wait()
        if b + AHEAD < count:
            for copy in load(b + AHEAD):
                copy.start()
        parts = []
        for c in range(3):
            start, end = (
                jnp.concatenate(
                    [
                        flat[pl.ds((c * seg + b * rows + 8 * k) * SUBLANES + 4 * h + n, 8, stride=SUBLANES), :]
                        for h in range(2)
                        for k in range(rows // 8)
                    ],
                    axis=0,
                )
                for n in (0, 3)
            )
            parts.append(jnp.where(low_lane, start, end))
        pieces = []
        for field in six_fields(parts[2], parts):
            pieces += list(split_value(field))
        both = jnp.dot(jnp.concatenate(pieces, axis=1), weights[...], preferred_element_type=jnp.float32)
        numbers = both[:, :LANES] + both[:, LANES:]
        for h in range(2):
            turned = numbers[h * rows : (h + 1) * rows].T
            numbers_ref[:, pl.ds(h * seg + b * rows, rows)] = turned[0:24]


HBM = pl.BlockSpec(memory_space=pl.ANY)
VMEM = pl.BlockSpec(memory_space=pltpu.VMEM)


def ends(view, seg):
    return pl.pallas_call(
        functools.partial(ends_kernel, seg),
        out_shape=(
            jax.ShapeDtypeStruct((3, seg, SUBLANES, LANES), jnp.float32),
            jax.ShapeDtypeStruct((24, 2 * seg), jnp.float32),
        ),
        in_specs=[HBM],
        out_specs=(VMEM, VMEM),
        scratch_shapes=[
            pltpu.VMEM((12 * LANES, 2 * LANES), jnp.bfloat16),
            pltpu.SemaphoreType.DMA((seg // LANES, 6)),
        ],
        compiler_params=pltpu.CompilerParams(vmem_limit_bytes=44 * 2**20),
        name="line_ends",
    )(view)


def x_kernel(seg, vel_ref, s_ref, sums_ref):
    reach = REACH_D
    first = low_rows()
    zero = jnp.zeros((SUBLANES, LANES), jnp.float32)
    start = ((zero,) * 6, (zero,) * 4)

    def advance(values, carry):
        sums, near = carry
        speed = SCALE * values[0]
        terms = six_fields(speed, values)
        bend = BETA * (near[3] + speed)
        found = [(sums[3 + c] + speed * sums[c]) + near[c] * bend for c in range(3)]
        return found, (tuple(term + ROOT_D * total for term, total in zip(terms, sums)), (*values, speed))

    def row(i):
        return [vel_ref[c, i] for c in range(3)]

    def other(i, keep_first):
        turned = [pltpu.roll(value, 4, axis=0) for value in row(i)]
        return [jnp.where(first, value, 0.0) if keep_first else jnp.where(first, 0.0, value) for value in turned]

    def forward(i, carry):
        found, carry = advance(row(i), carry)
        for c in range(3):
            s_ref[c, i] = found[c]
        return carry

    def backward(k, carry):
        i = seg - 1 - k
        found, carry = advance(row(i), carry)
        for c in range(3):
            s_ref[c, i] = found[c] - s_ref[c, i]
        return carry

    carry = lax.fori_loop(0, reach, lambda i, k: advance(other(seg - reach + i, False), k)[1], start, unroll=8)
    carry = lax.fori_loop(0, seg, forward, carry, unroll=32)
    for field in range(6):
        sums_ref[0, field] = carry[0][field]
    carry = lax.fori_loop(0, reach, lambda i, k: advance(other(reach - 1 - i, True), k)[1], start, unroll=8)
    carry = lax.fori_loop(0, seg, backward, carry, unroll=32)
    for field in range(6):
        sums_ref[1, field] = carry[0][field]


def x_part(vel, seg):
    points = 3 * 2 * seg * 4 * LANES
    return pl.pallas_call(
        functools.partial(x_kernel, seg),
        out_shape=(
            jax.ShapeDtypeStruct(vel.shape, jnp.float32),
            jax.ShapeDtypeStruct((2, 6, SUBLANES, LANES), jnp.float32),
        ),
        in_specs=[VMEM],
        out_specs=(VMEM, VMEM),
        compiler_params=pltpu.CompilerParams(vmem_limit_bytes=16 * 2**20),
        cost_estimate=pl.CostEstimate(flops=60 * points, bytes_accessed=8 * points, transcendentals=0),
        name="x_slopes",
    )(vel)


def z_kernel(
    seg, vel_ref, sx_ref, xsums_ref, table_ref, zl_ref, zr_ref,
    sbuf, ups_ref, downs_ref, one_ref, two_ref,
    weights, turn, halo_hi, halo_lo, pack,
):
    far = REACH_F
    step_rows = STEP_ROWS
    rows = 2 * step_rows
    first = low_rows()
    flat = vel_ref.reshape(3 * seg * SUBLANES, LANES)

    for part in range(2):
        high, low = split_value(table_ref[part * LANES : (part + 1) * LANES, :])
        for copy in range(2):
            at = pl.ds((2 * part + copy) * LANES, LANES)
            weights[at, 0:LANES] = high
            weights[at, LANES:] = low

    lane = lax.broadcasted_iota(jnp.int32, (LANES, LANES), 1)
    outer_lane = (lane >= LANES - 2) | (lane < 2)
    from_before = lax.broadcasted_iota(jnp.int32, (24, LANES), 0) % 4 < 2
    turn[24:, :] = jnp.zeros((LANES - 24, LANES), jnp.float32)
    for part in range(2 * seg // LANES):
        at = pl.ds(part * LANES, LANES)
        turn[0:24, :] = jnp.where(from_before, zl_ref[:, at], zr_ref[:, at])
        numbers = turn[...].T
        for field in range(6):
            moved = pltpu.roll(numbers, LANES - 2 - 4 * field, axis=1)
            high, low = split_value(jnp.where(outer_lane, moved, 0.0))
            halo_hi[field, at, :] = high
            halo_lo[field, at, :] = low

    along_x = sx_ref.reshape(3 * seg * SUBLANES, LANES)
    low_lane = jnp.where(low_lanes(rows), 1.0, 0.0).astype(jnp.bfloat16) > 0.5

    def strided(c, xi, n):
        return jnp.concatenate(
            [
                flat[pl.ds((c * seg + xi + 8 * k) * SUBLANES + 4 * h + n, 8, stride=SUBLANES), :]
                for h in range(2)
                for k in range(step_rows // 8)
            ],
            axis=0,
        )

    def build(step):
        store = {}
        xi = pl.multiple_of(step * step_rows, step_rows)
        along = [[strided(c, xi, n) for c in range(3)] for n in range(4)]
        for field in range(6):
            halves = []
            for n in range(4):
                value = along[n][field % 3]
                halves.append(split_value(along[n][2] * value if field >= 3 else value))
            for which, halo in ((0, halo_hi), (1, halo_lo)):
                outer = jnp.concatenate(
                    [halo[field, pl.ds(pl.multiple_of(h * seg + xi, 16), step_rows), :] for h in range(2)], axis=0
                )
                line = [outer] + [pair[which] for pair in halves] + [outer]
                for n in range(4):
                    at = pl.ds(((field % 3 * 4 + n) * 2 + field // 3) * rows, rows)
                    store[(field % 3 * 4 + n) * 2 + field // 3, which] = line[n + 1]
                    store[(field % 3 * 4 + n) * 2 + field // 3, 2 + which] = jnp.where(low_lane, line[n + 2], line[n])
        return jnp.concatenate([jnp.concatenate([store[q, p] for p in range(4)], axis=1) for q in range(24)], axis=0)

    def finish(step, both):
        xi = pl.multiple_of(step * step_rows, step_rows)
        alongs = [strided(2, xi, n) for n in range(4)]
        for c in range(3):
            for n in range(4):
                along = alongs[n]
                base = (c * 4 + n) * 2 * rows
                plain = both[base : base + rows]
                mixed = both[base + rows : base + 2 * rows]
                term = (mixed[:, :LANES] + mixed[:, LANES:]) + along * (plain[:, :LANES] + plain[:, LANES:])
                for h in range(2):
                    for k in range(step_rows // 8):
                        at = (c * seg + xi + 8 * k) * SUBLANES + 4 * h + n
                        piece = h * (step_rows // 8) + k
                        at = pl.ds(at, 8, stride=SUBLANES)
                        sbuf[at, :] = term[piece * 8 : piece * 8 + 8] + along_x[at, :]

    zero = jnp.zeros((SUBLANES, LANES), jnp.float32)

    def block(step, _):
        finish(step, jnp.dot(build(step), weights[...], preferred_element_type=jnp.float32))
        return 0

    lax.fori_loop(0, seg // step_rows, block, 0)

    def row_of(c, row):
        at = pl.ds(pl.multiple_of((c * seg + row) * SUBLANES, SUBLANES), SUBLANES)
        return sbuf[at, :]

    def sums_of(k, sums):
        ups, downs = sums
        ups = tuple(row_of(c, far - 1 - k) + ROOT_F * ups[c] for c in range(3))
        downs = tuple(row_of(c, seg - far + k) + ROOT_F * downs[c] for c in range(3))
        return ups, downs

    ups, downs = lax.fori_loop(0, far, sums_of, ((zero,) * 3,) * 2, unroll=8)
    for c in range(3):
        ups_ref[c] = ups[c]
        downs_ref[c] = downs[c]

    for field in range(6):
        pack[field] = jnp.where(first, xsums_ref[1, field], xsums_ref[0, field])
    for c in range(3):
        pack[6 + c] = jnp.where(first, vel_ref[c, 0], vel_ref[c, seg - 1])
        pack[9 + c] = jnp.where(first, ups[c], downs[c])
        pack[12 + c] = jnp.where(first, row_of(c, 0), row_of(c, seg - 1))
        pack[15 + c] = jnp.where(first, row_of(c, 1), row_of(c, seg - 2))
    weighted = zero
    for k in reversed(range(REACH_D)):
        weighted = jnp.where(first, vel_ref[0, k], vel_ref[0, seg - 1 - k]) + (ROOT_F * ROOT_D) * weighted
    pack[18] = SCALE * weighted
    pack[19] = SCALE * jnp.where(first, vel_ref[0, 1], vel_ref[0, seg - 2])
    even = lax.axis_index("gx") % 2 == 0
    one_ref[...] = jnp.where(even, pack[:, 4:8, :], pack[:, 0:4, :])
    two_ref[...] = jnp.where(even, pack[:, 0:4, :], pack[:, 4:8, :])


def z_part(vel, local, xsums, seg, before_z, after_z):
    side = jax.ShapeDtypeStruct((20, 4, LANES), jnp.float32)
    return pl.pallas_call(
        functools.partial(z_kernel, seg),
        out_shape=(
            jax.ShapeDtypeStruct((3 * seg * SUBLANES, LANES), jnp.float32),
            jax.ShapeDtypeStruct((3, SUBLANES, LANES), jnp.float32),
            jax.ShapeDtypeStruct((3, SUBLANES, LANES), jnp.float32),
            side,
            side,
        ),
        in_specs=[VMEM] * 6,
        out_specs=(VMEM,) * 5,
        scratch_shapes=[
            pltpu.VMEM((4 * LANES, 2 * LANES), jnp.bfloat16),
            pltpu.VMEM((LANES, LANES), jnp.float32),
            pltpu.VMEM((6, 2 * seg, LANES), jnp.bfloat16),
            pltpu.VMEM((6, 2 * seg, LANES), jnp.bfloat16),
            pltpu.VMEM((20, SUBLANES, LANES), jnp.float32),
        ],
        compiler_params=pltpu.CompilerParams(vmem_limit_bytes=28 * 2**20),
        name="z_slopes",
    )(vel, local, xsums, jnp.asarray(line_table()), before_z, after_z)


def filter_kernel(seg, s_ref, ups_ref, downs_ref, o_ref, rim_ref, o_buf, sems):
    size = seg // PIECES
    turns = size // GROUP
    warm_group = REACH_F // turns
    first = low_rows()

    def term(c, row):
        at = pl.ds(pl.multiple_of((c * seg + row) * SUBLANES, SUBLANES), SUBLANES)
        return s_ref[at, :]

    def to_second(value):
        return jnp.where(first, 0.0, pltpu.roll(value, 4, axis=0))

    def to_first(value):
        return jnp.where(first, pltpu.roll(value, 4, axis=0), 0.0)

    def down_row(here, carry):
        found, out = [], []
        for c in range(3):
            down, scaled1, scaled2, one, two, three, four = carry[c]
            scaled = ROOT_F * down
            taps = TAP0 * two + TAP1 * (one + three) + TAP2 * (here[c] + four)
            found.append(scaled2 + taps)
            out.append((here[c] + scaled, scaled, scaled1, here[c], one, two, three))
        return found, tuple(out)

    def down_rows(b, i, carry):
        low = b * size + 2 + GROUP * i
        count = GROUP
        lines = [[term(c, low + k) for c in range(3)] for k in range(count)]
        results = []
        for here in lines:
            found, carry = down_row(here, carry)
            results.append(found)
        for k in range(count):
            for c in range(3):
                o_buf[c, low + k - 2] = results[k][c]
        return carry

    def warm_rows(b, i, ups):
        top = (b + 1) * size + REACH_F - 1 - warm_group * i
        lines = [[term(c, top - k) for c in range(3)] for k in range(warm_group)]
        for here in lines:
            ups = tuple(here[c] + ROOT_F * ups[c] for c in range(3))
        return ups

    def up_rows(b, i, ups):
        low = (b + 1) * size - GROUP * (i + 1)
        order = list(reversed(range(GROUP)))
        here = {(k, c): term(c, low + k) for k in order for c in range(3)}
        found = {(k, c): o_buf[c, low + k] for k in order for c in range(3)}
        for k in order:
            ups = tuple(here[k, c] + ROOT_F * ups[c] for c in range(3))
            for c in range(3):
                found[k, c] = found[k, c] + ups[c]
        for k in order:
            for c in range(3):
                o_buf[c, low + k] = found[k, c]
        return ups

    def store(b):
        at = pl.ds(b * size, size)
        edge = RIM // size
        return [
            pltpu.make_async_copy(o_buf.at[c, at, pl.ds(4 * h, 4)], o_ref.at[c, h, at], sems.at[b, 2 * c + h])
            for c in range(3)
            for h in range(2)
            if (b >= edge if h == 0 else b < PIECES - edge)
        ]

    zero = jnp.zeros((SUBLANES, LANES), jnp.float32)
    zeros = (zero,) * 3
    carry = tuple(
        (
            to_second(downs_ref[c]), zero, zero,
            to_second(term(c, seg - 1)), to_second(term(c, seg - 2)), zero, zero,
        )
        for c in range(3)
    )
    for k in range(2):
        carry = down_row([term(c, k) for c in range(3)], carry)[1]
    last = tuple(to_first(ups_ref[c]) for c in range(3))

    def opening(i, state):
        carry, warmed = state
        return down_rows(0, i, carry), warm_rows(0, i, warmed)

    carry, warmed = lax.fori_loop(0, turns, opening, (carry, zeros), unroll=4)
    for b in range(PIECES):
        if b < PIECES - 2:

            def body(i, state, b=b):
                carry, warmed, ups = state
                return down_rows(b + 1, i, carry), warm_rows(b + 1, i, warmed), up_rows(b, i, ups)

            carry, warmed, _ = lax.fori_loop(0, turns, body, (carry, zeros, warmed), unroll=4)
        elif b == PIECES - 2:

            def body(i, state, b=b):
                carry, ups = state
                return down_rows(b + 1, i, carry), up_rows(b, i, ups)

            carry, _ = lax.fori_loop(0, turns - 1, body, (carry, warmed), unroll=4)
            _ = up_rows(b, turns - 1, _)
            low = seg - GROUP + 2
            for k in range(GROUP):
                row = low + k
                here = [term(c, row) if row < seg else to_first(term(c, row - seg)) for c in range(3)]
                found, carry = down_row(here, carry)
                for c in range(3):
                    o_buf[c, row - 2] = found[c]
        else:
            lax.fori_loop(0, turns, lambda i, ups: up_rows(PIECES - 1, i, ups), last, unroll=4)
        for copy in store(b):
            copy.start()

    def to_rim(k, _):
        for c in range(3):
            rim_ref[c, k] = jnp.where(first, o_buf[c, k], o_buf[c, seg - 1 - k])
        return 0

    lax.fori_loop(0, RIM, to_rim, 0, unroll=8)
    for b in range(PIECES):
        for copy in store(b):
            copy.wait()


def filter_part(terms, ups, downs, seg):
    points = 3 * 2 * seg * 4 * LANES
    return pl.pallas_call(
        functools.partial(filter_kernel, seg),
        out_shape=(
            jax.ShapeDtypeStruct((3, 2, seg, 4, LANES), jnp.float32),
            jax.ShapeDtypeStruct((3, RIM, SUBLANES, LANES), jnp.float32),
        ),
        in_specs=[VMEM] * 3,
        out_specs=(HBM, VMEM),
        scratch_shapes=[
            pltpu.VMEM((3, seg, SUBLANES, LANES), jnp.float32),
            pltpu.SemaphoreType.DMA((PIECES, 6)),
        ],
        compiler_params=pltpu.CompilerParams(vmem_limit_bytes=24 * 2**20),
        cost_estimate=pl.CostEstimate(flops=20 * points, bytes_accessed=12 * points, transcendentals=0),
        name="compact_filter",
    )(terms, ups, downs)


def rim_kernel(seg, o_in, rim_ref, vel_ref, xsums_ref, one_ref, two_ref, o_ref, edge, top, bottom, sems):
    del o_in
    reach = REACH_D
    first = low_rows()
    sign = jnp.where(first, -1.0, 1.0).astype(jnp.float32)
    even = lax.axis_index("gx") % 2 == 0
    edge[:, 0:4, :] = jnp.where(even, two_ref[...], one_ref[...])
    edge[:, 4:8, :] = jnp.where(even, one_ref[...], two_ref[...])
    own = [jnp.where(first, xsums_ref[1, field], xsums_ref[0, field]) for field in range(6)]
    raw = [jnp.where(first, vel_ref[c, 0], vel_ref[c, seg - 1]) for c in range(3)]
    speeds = [SCALE * jnp.where(first, vel_ref[0, k], vel_ref[0, seg - 1 - k]) for k in range(reach)]
    next_to, second = SCALE * edge[6], edge[19]
    for c in range(3):
        bend = (BETA * raw[c]) * (speeds[0] + next_to)
        close = edge[12 + c] - sign * ((own[3 + c] + next_to * own[c]) + bend)
        further = edge[15 + c] - sign * (ROOT_D * (own[3 + c] + second * own[c]))
        gain = 1.0 / (1.0 - ROOT_F * ROOT_D)
        total = edge[9 + c] - sign * ((gain * own[3 + c] + edge[18] * own[c]) + bend)
        change = [
            (sign * ROOT_D**k) * (edge[3 + c] + speeds[k] * edge[c]) for k in range(reach)
        ]
        change[0] = change[0] + sign * ((BETA * edge[6 + c]) * (next_to + speeds[0]))
        line = [further, close] + change + [jnp.zeros_like(close)] * 4
        ups = [None] * reach
        up = jnp.zeros_like(close)
        for k in reversed(range(reach)):
            up = change[k] + ROOT_F * up
            ups[k] = up
        for k in range(RIM):
            scaled = ROOT_F * total
            found = scaled
            if k < reach + 2:
                here = line[k + 2]
                taps = TAP0 * here + TAP1 * (line[k + 1] + line[k + 3]) + TAP2 * (line[k] + line[k + 4])
                found = found + taps
            if k < reach:
                found = found + ups[k]
                total = change[k] + scaled
            else:
                total = scaled
            fixed = rim_ref[c, k] + found
            top[c, k] = fixed
            bottom[c, RIM - 1 - k] = fixed
        pltpu.make_async_copy(top.at[c, :, pl.ds(0, 4)], o_ref.at[c, 0, pl.ds(0, RIM)], sems.at[c, 0]).start()
        pltpu.make_async_copy(
            bottom.at[c, :, pl.ds(4, 4)], o_ref.at[c, 1, pl.ds(seg - RIM, RIM)], sems.at[c, 1]
        ).start()
    for c in range(3):
        pltpu.make_async_copy(top.at[c, :, pl.ds(0, 4)], o_ref.at[c, 0, pl.ds(0, RIM)], sems.at[c, 0]).wait()
        pltpu.make_async_copy(
            bottom.at[c, :, pl.ds(4, 4)], o_ref.at[c, 1, pl.ds(seg - RIM, RIM)], sems.at[c, 1]
        ).wait()


def rim_part(out, rim, vel, xsums, one, two, seg):
    return pl.pallas_call(
        functools.partial(rim_kernel, seg),
        out_shape=jax.ShapeDtypeStruct(out.shape, jnp.float32),
        in_specs=[HBM] + [VMEM] * 5,
        out_specs=HBM,
        input_output_aliases={0: 0},
        scratch_shapes=[
            pltpu.VMEM((20, SUBLANES, LANES), jnp.float32),
            pltpu.VMEM((3, RIM, SUBLANES, LANES), jnp.float32),
            pltpu.VMEM((3, RIM, SUBLANES, LANES), jnp.float32),
            pltpu.SemaphoreType.DMA((3, 2)),
        ],
        compiler_params=pltpu.CompilerParams(vmem_limit_bytes=16 * 2**20),
        name="rim",
    )(out, rim, vel, xsums, one, two)


def ring(axis):
    count = lax.axis_size(axis)
    forward = [(i, (i + 1) % count) for i in range(count)]
    return forward, [(target, source) for source, target in forward]


def pairs(axis):
    count = lax.axis_size(axis)
    one = [(i, i + 1 if i % 2 == 0 else i - 1) for i in range(count)]
    two = [(i, (i - 1 if i % 2 == 0 else i + 1) % count) for i in range(count)]
    return one, two


def blocked(velocity):
    seg = velocity.shape[1] // 2
    vel, numbers = ends(velocity.reshape(3, 2, seg, 4, LANES), seg)
    forward, backward = ring("gz")
    before_z = lax.ppermute(numbers, "gz", forward)
    after_z = lax.ppermute(numbers, "gz", backward)
    local, xsums = x_part(vel, seg)
    terms, ups, downs, one, two = z_part(vel, local, xsums, seg, before_z, after_z)
    first_swap, second_swap = pairs("gx")
    one = lax.ppermute(one, "gx", first_swap)
    two = lax.ppermute(two, "gx", second_swap)
    out, rim = filter_part(terms, ups, downs, seg)
    return rim_part(out, rim, vel, xsums, one, two, seg).reshape(velocity.shape)


def with_halo(block, sides, width):
    for axis, dim in sides:
        count = lax.axis_size(axis)
        forward = [(i, i + 1) for i in range(count - 1)]
        forward.append((count - 1, 0))
        backward = [(target, source) for source, target in forward]
        low = lax.ppermute(
            lax.slice_in_dim(block, block.shape[dim] - width, None, axis=dim), axis, forward
        )
        high = lax.ppermute(lax.slice_in_dim(block, 0, width, axis=dim), axis, backward)
        block = jnp.concatenate([low, block, high], axis=dim)
    return block


def tables(length, alpha):
    lower_diag = jnp.concatenate(
        [jnp.zeros((1,), jnp.float32), jnp.full((length - 1,), alpha, jnp.float32)]
    )
    upper_diag = jnp.concatenate(
        [jnp.full((length - 1,), alpha, jnp.float32), jnp.zeros((1,), jnp.float32)]
    )
    main_diag = jnp.ones((length,), jnp.float32)
    identity = jnp.eye(length, dtype=jnp.float32)
    inverse = lax.linalg.tridiagonal_solve(lower_diag, main_diag, upper_diag, identity)
    left_col = alpha * inverse[:, 0]
    right_col = alpha * inverse[:, length - 1]
    coupling = alpha * inverse[0, 0]
    return (inverse, left_col, right_col, coupling)


def offset_slice(extended, offset, length, direction, base=3):
    return lax.slice_in_dim(extended, base + offset, base + offset + length, axis=direction)


def slope_rhs(extended, length, direction, base=3):
    rhs = (
        COEF_A
        * 0.5
        * (
            offset_slice(extended, 1, length, direction, base)
            - offset_slice(extended, -1, length, direction, base)
        )
    )
    return rhs + COEF_B * 0.25 * (
        offset_slice(extended, 2, length, direction, base)
        - offset_slice(extended, -2, length, direction, base)
    )


def smooth_rhs(extended, length, direction, base=3):
    coefficients = filter_coefficients()
    rhs = coefficients[0] * offset_slice(extended, 0, length, direction, base)
    for offset in range(1, 4):
        rhs = rhs + 0.5 * coefficients[offset] * (
            offset_slice(extended, offset, length, direction, base)
            + offset_slice(extended, -offset, length, direction, base)
        )
    return rhs


def wrap_pad(values, direction):
    length = values.shape[direction]
    return jnp.concatenate(
        [
            lax.slice_in_dim(values, length - 3, length, axis=direction),
            values,
            lax.slice_in_dim(values, 0, 3, axis=direction),
        ],
        axis=direction,
    )


def apply_along(inverse, values, direction):
    rotated = jnp.tensordot(
        inverse, values, axes=([1], [direction]), precision=lax.Precision.HIGHEST
    )
    return jnp.moveaxis(rotated, 0, direction)


def end_values(partial_value, direction):
    length = partial_value.shape[direction]
    first_val = lax.slice_in_dim(partial_value, 0, 1, axis=direction)
    last_val = lax.slice_in_dim(partial_value, length - 1, length, axis=direction)
    return (first_val, last_val)


def corrected(partial_value, prev_last, next_first, table, direction):
    inverse, left_col, right_col, coupling = table
    first_val, last_val = end_values(partial_value, direction)
    factor_inv = 1.0 / (1.0 - coupling * coupling)
    left_value = (prev_last - coupling * first_val) * factor_inv
    right_value = (next_first - coupling * last_val) * factor_inv
    dims_list = [1] * partial_value.ndim
    dims_list[direction] = partial_value.shape[direction]
    return (
        partial_value
        - left_col.reshape(dims_list) * left_value
        - right_col.reshape(dims_list) * right_value
    )


def extend_x(values):
    return with_halo(values, (("gx", 1),), 3)


def solve_x(rhs, table):
    partial_value = apply_along(table[0], rhs, 1)
    first_val, last_val = end_values(partial_value, 1)
    beside = with_halo(jnp.concatenate([first_val, last_val], axis=1), (("gx", 1),), 1)
    return corrected(partial_value, beside[:, 0:1], beside[:, 3:4], table, 1)


def solve_blocks(rhs, table):
    dims_list = rhs.shape
    blocks = rhs.reshape(dims_list[:-1] + (dims_list[-1] // block_len, block_len))
    last_dim = blocks.ndim - 1
    partial_value = apply_along(table[0], blocks, last_dim)
    first_val, last_val = end_values(partial_value, last_dim)
    prev_last = jnp.roll(last_val, 1, axis=last_dim - 1)
    next_first = jnp.roll(first_val, -1, axis=last_dim - 1)
    return corrected(partial_value, prev_last, next_first, table, last_dim).reshape(dims_list)


def whole_z_part(velocity):
    slope_z = tables(block_len, ALPHA_D)
    pencil = lax.all_to_all(velocity, "gz", split_axis=1, concat_axis=3, tiled=True)
    along_z = pencil[2:3]
    fields = jnp.concatenate([pencil, along_z * pencil], axis=0)
    slopes = solve_blocks(slope_rhs(wrap_pad(fields, 3), fields.shape[3], 3), slope_z)
    local_terms = slopes[3:] + along_z * slopes[:3]
    return lax.all_to_all(local_terms, "gz", split_axis=3, concat_axis=1, tiled=True)


def per_device(velocity):
    width_x = velocity.shape[1]
    slope_x = tables(width_x, ALPHA_D)
    smooth_x = tables(width_x, ALPHA_F)
    along_x = velocity[0:1]
    rim_source = jnp.concatenate([velocity, along_x * velocity], axis=0)
    padded = extend_x(rim_source)
    slopes_x = solve_x(slope_rhs(padded, width_x, 1), slope_x)
    x_terms = slopes_x[3:] + along_x * slopes_x[:3]
    z_terms = whole_z_part(velocity)
    combined = 0.5 * (x_terms + z_terms)
    smoothed = solve_x(smooth_rhs(extend_x(combined), width_x, 1), smooth_x)
    return -smoothed


def per_block(velocity):
    _, rows, planes, columns = velocity.shape
    fits = planes == 1 and columns == 4 * LANES and rows % 1024 == 0 and lax.axis_size("gx") % 2 == 0
    return blocked(velocity) if fits else per_device(velocity)


def solution(mesh):
    return jax.shard_map(
        per_block,
        mesh=mesh,
        in_specs=(P(None, "gx", None, "gz"),),
        out_specs=P(None, "gx", None, "gz"),
        check_vma=False,
    )
```
